32 devices in a mesh: seq: 8 (over z, x), head: 4 (over y, core).
Axes of the slice: x: 2, y: 2, z: 4, core: 2. Of those that a mesh axis runs over, the one named last changes fastest.
Arguments:
- hidden_in: bfloat16 [2048, 2048], P('seq'), may hold values from -6 to 6
- w_qk: bfloat16 [2048, 2, 2048], P(None, None, 'head'), may hold values from -0.125 to 0.125
- w_value: bfloat16 [2048, 4096], P(None, 'head'), may hold values from -0.125 to 0.125
- w_outgate: bfloat16 [2048, 4096], P(None, 'head'), may hold values from -0.125 to 0.125
- w_ba: bfloat16 [2048, 2, 32], P(None, None, 'head'), may hold values from -0.125 to 0.125
- conv_qk: bfloat16 [4, 2, 2048], P(None, None, 'head'), may hold values from -3 to 3
- conv_value: bfloat16 [4, 4096], P(None, 'head'), may hold values from -3 to 3
- hist_qk: bfloat16 [3, 2, 2048], P(None, None, 'head'), may hold values from -6 to 6
- hist_value: bfloat16 [3, 4096], P(None, 'head'), may hold values from -6 to 6
- a_log: float32 [32], P('head'), may hold values from -11 to -3
- dt_bias: float32 [32], P('head'), may hold values from -1 to 1
- beta_bias: float32 [32], P('head'), may hold values from -1 to 1
- state_in: float32 [32, 128, 128], P('head'), may hold values from -0.6 to 0.6
- norm_gain: float32 [128], replicated, may hold values from 0.5 to 1.5
- w_out: bfloat16 [4096, 2048], P('head'), may hold values from -0.09375 to 0.09375
Outputs:
- mixed: bfloat16 [2048, 2048], P('seq', 'head')
- checkpoints: float32 [8, 32, 128, 128], P('seq', 'head')
The draws below stay inside these ranges and needn't reach their ends.
All inputs are finite; a program needn't handle non-finite values.
Results may differ from the reference program's by a relative error of at most 0.015.
Values may be sent and summed in bfloat16 or wider, within the bound.
No kernel may reach another device: no remote copies, remote signals or barrier semaphores. Data moves between devices by JAX's collectives and lax.ppermute only.
A program may use at most 64 MiB of HBM per device.

```python
import jax
import jax.numpy as jnp
from jax import lax

D = 2048
HK = 16
HV = 32
KEY_HEAD_SIZE = 128
DV = 128
KC = 4
TOK_DEV = 256
KEYW = 2048
VALW = 4096
TOKENS = 2048
N_SEQ = 8
N_HEAD = 4


def block_levels(stream_key, shape, pieces, low, high):
    def one(dim, shards_of):
        heights = jax.random.uniform(jax.random.fold_in(jax.random.fold_in(stream_key, 6), dim), (shards_of,), jnp.float32, low / len(pieces), high / len(pieces))
        return jnp.repeat(jnp.exp(heights), shape[dim] // shards_of).reshape((-1,) + (1,) * (len(shape) - dim - 1))

    level = one(*pieces[0])
    for cut in pieces[1:]:
        level = level * one(*cut)
    return level


def centred(own_key, extent, spread, reach, split=(), dtype=jnp.bfloat16):
    level = block_levels(own_key, extent, split, -0.22, 0.18) if split else 1.0
    values = jax.random.normal(own_key, extent, jnp.float32) * spread * level
    return jnp.minimum(jnp.maximum(values, -reach), reach).astype(dtype)


def setup_inputs(seed: int = 0) -> dict:
    key_of = jax.random.split(jax.random.key(seed), 16)
    return {
        "hidden_in": centred(key_of[0], (TOKENS, D), 1.0, 6.0, ((0, 8),)),
        "w_qk": centred(key_of[1], (D, 2, KEYW), D ** -0.5, 0.125, ((2, 4),)),
        "w_value": centred(key_of[2], (D, VALW), D ** -0.5, 0.125, ((1, 4),)),
        "w_outgate": centred(key_of[3], (D, VALW), D ** -0.5, 0.125, ((1, 4),)),
        "w_ba": centred(key_of[4], (D, 2, HV), D ** -0.5, 0.125, ((2, 4),)),
        "conv_qk": centred(key_of[5], (KC, 2, KEYW), 0.5, 3.0, ((2, 4),)),
        "conv_value": centred(key_of[6], (KC, VALW), 0.5, 3.0, ((1, 4),)),
        "hist_qk": centred(key_of[7], (KC - 1, 2, KEYW), 1.0, 6.0, ((2, 4),)),
        "hist_value": centred(key_of[8], (KC - 1, VALW), 1.0, 6.0, ((1, 4),)),
        "a_log": jnp.clip(-11.0 + 8.0 * jax.random.uniform(key_of[9], (HV,), jnp.float32) ** block_levels(key_of[9], (HV,), ((0, 4),), -0.2, 0.2), -11.0, -3.0),
        "dt_bias": jnp.clip(jax.random.uniform(key_of[10], (HV,), jnp.float32, -1.0, 1.0) * block_levels(key_of[10], (HV,), ((0, 4),), -0.4, 0.0), -1.0, 1.0),
        "beta_bias": jnp.clip(jax.random.uniform(key_of[11], (HV,), jnp.float32, -1.0, 1.0) * block_levels(key_of[11], (HV,), ((0, 4),), -0.4, 0.0), -1.0, 1.0),
        "state_in": centred(key_of[12], (HV, KEY_HEAD_SIZE, DV), 0.1, 0.6, ((0, 4),), jnp.float32),
        "norm_gain": jnp.clip(1.0 + 0.1 * jax.random.normal(key_of[13], (DV,), jnp.float32), 0.5, 1.5),
        "w_out": centred(key_of[14], (VALW, D), VALW ** -0.5, 0.09375, ((0, 4),)),
    }


exact_setting = lax.Precision.HIGHEST

def stored(values):
    return lax.optimization_barrier(values.astype(jnp.bfloat16))

def unit_rows(values):
    return values * lax.rsqrt(lax.optimization_barrier(jnp.sum(values * values, axis=-1, keepdims=True)) + 1e-06)

def causal_filter(history, present, weight):
    joined = jnp.concatenate([history, present], 0).astype(jnp.float32)
    count = present.shape[0]
    total = jnp.zeros(present.shape, jnp.float32)
    for offset in range(weight.shape[0]):
        total = total + weight[offset].astype(jnp.float32) * joined[offset:offset + count]
    return jax.nn.silu(total)

def reference(hidden_in, w_qk, w_value, w_outgate, w_ba, conv_qk, conv_value, hist_qk, hist_value, a_log, dt_bias, beta_bias, state_in, norm_gain, w_out):
    total_rows = hidden_in.shape[0]
    pre_qk = stored(jnp.dot(hidden_in, w_qk.reshape(D, 2 * KEYW), preferred_element_type=jnp.float32))
    pre_value = stored(jnp.dot(hidden_in, w_value, preferred_element_type=jnp.float32))
    mixed_qk = causal_filter(hist_qk.reshape(KC - 1, 2 * KEYW), pre_qk, conv_qk.reshape(KC, 2 * KEYW)).reshape(total_rows, 2, HK, KEY_HEAD_SIZE)
    values = causal_filter(hist_value, pre_value, conv_value).reshape(total_rows, HV, DV)
    queries = jnp.repeat(unit_rows(mixed_qk[:, 0]) * KEY_HEAD_SIZE ** (-0.5), HV // HK, axis=1)
    keys = jnp.repeat(unit_rows(mixed_qk[:, 1]), HV // HK, axis=1)
    gates_in = stored(jnp.dot(hidden_in, w_ba.reshape(D, 2 * HV), preferred_element_type=jnp.float32)).astype(jnp.float32).reshape(total_rows, 2, HV)
    strength = jax.nn.sigmoid(gates_in[:, 0] + beta_bias)
    log_decay = -jnp.exp(a_log) * jax.nn.softplus(gates_in[:, 1] + dt_bias)

    def token_step(current_state, inputs):
        query_vector, key_vector, value_row, beta_row, decay_row = inputs
        decayed_state = jnp.exp(decay_row)[:, None, None] * current_state
        predicted_value = jnp.einsum('xqf,xq->xf', decayed_state, key_vector, precision=exact_setting)
        written = beta_row[:, None] * (value_row - predicted_value)
        current_state = decayed_state + key_vector[:, :, None] * written[:, None, :]
        return (current_state, jnp.einsum('xqf,xq->xf', current_state, query_vector, precision=exact_setting))

    def block_step(current_state, block):
        current_state, outs = lax.scan(token_step, current_state, block)
        return (current_state, (outs, current_state))
    shaped = tuple((t.reshape((N_SEQ, TOK_DEV) + t.shape[1:]) for t in (queries, keys, values, strength, log_decay)))
    final_state, (outputs, checkpoints) = lax.scan(block_step, state_in.astype(jnp.float32), shaped)
    outputs = outputs.reshape(total_rows, HV, DV)
    gate_z = stored(jnp.dot(hidden_in, w_outgate, preferred_element_type=jnp.float32)).astype(jnp.float32).reshape(total_rows, HV, DV)
    scale = lax.rsqrt(lax.optimization_barrier(jnp.mean(outputs * outputs, axis=-1, keepdims=True)) + 1e-06)
    normed = (outputs * scale * norm_gain * jax.nn.silu(gate_z)).astype(jnp.bfloat16).reshape(total_rows, VALW)
    group = VALW // N_HEAD
    total = jnp.zeros((total_rows, D), jnp.float32)
    for member in range(N_HEAD):
        piece = jnp.dot(normed[:, member * group:(member + 1) * group], w_out[member * group:(member + 1) * group], preferred_element_type=jnp.float32)
        total = total + lax.optimization_barrier(piece.astype(jnp.bfloat16)).astype(jnp.float32)
    return (total.astype(jnp.bfloat16), checkpoints)
```

```python
import functools

import jax
import jax.numpy as jnp
from jax import lax
from jax.experimental import pallas as pl
from jax.experimental.pallas import tpu as pltpu
from jax.sharding import PartitionSpec as P

KD = 128
DV = 128
HALF = 128
HALO = 8
F32 = jnp.float32
BF16 = jnp.bfloat16
VMEM = pl.BlockSpec(memory_space=pltpu.VMEM)
SMEM = pl.BlockSpec(memory_space=pltpu.SMEM)


def dot(left, right):
    return jnp.dot(left, right, preferred_element_type=F32)


def dot_nt(left, right):
    return lax.dot_general(left, right, (((1,), (1,)), ((), ())), preferred_element_type=F32)


def split(values):
    high = values.astype(BF16)
    return high, (values - high.astype(F32)).astype(BF16)


def fine_dot(left, right):
    left_hi, left_lo = split(left)
    right_hi, right_lo = split(right)
    return dot(left_hi, right_hi) + (dot(left_hi, right_lo) + dot(left_lo, right_hi))


def silu(values):
    return values / (1.0 + jnp.exp(-values))


def unit_rows(values):
    return values * lax.rsqrt(jnp.sum(values * values, axis=-1, keepdims=True) + 1e-06)


def conv_rows(block, history, weight, first):
    rows = block.shape[0] - HALO
    taps = weight.shape[0]
    start = HALO - (taps - 1)
    halo = jnp.where(first, history, block[:HALO])
    joined = jnp.concatenate([halo, block[HALO:]], 0)
    total = weight[0:1] * joined[start : start + rows]
    for tap in range(1, taps):
        total = total + weight[tap : tap + 1] * joined[start + tap : start + tap + rows]
    return silu(total)


def call(kernel, out_shape, in_specs, flops, moved, scratch=()):
    return pl.pallas_call(
        kernel,
        out_shape=out_shape,
        in_specs=in_specs,
        out_specs=jax.tree.map(lambda _: VMEM, out_shape),
        scratch_shapes=list(scratch),
        compiler_params=pltpu.CompilerParams(vmem_limit_bytes=40 << 20),
        cost_estimate=pl.CostEstimate(flops=flops, bytes_accessed=moved, transcendentals=0),
    )


def shape(dims, dtype):
    return jax.ShapeDtypeStruct(dims, dtype)


def prepare_kernel(
    place, qk, value, gates, hist_qk, hist_value, conv_qk, conv_value, params,
    keys_out, solved_out, maps_out, send_out, rows_out, cols_out,
):
    heads = gates.shape[1]
    rows = gates.shape[2]
    key_heads = heads // 2
    first = place[0] == 0
    bit = place[1]
    strength = jax.nn.sigmoid(gates[0].astype(F32) + params[:, 2:3])
    decay_in = gates[1].astype(F32) + params[:, 1:2]
    soft = jnp.maximum(decay_in, 0.0) + jnp.log1p(jnp.exp(-jnp.abs(decay_in)))
    log_decay = -jnp.exp(params[:, 0:1]) * soft
    line = lax.broadcasted_iota(jnp.int32, (rows, rows), 0)
    across = lax.broadcasted_iota(jnp.int32, (rows, rows), 1)
    upper = jnp.where(line <= across, 1.0, 0.0).astype(BF16)
    high, low = split(log_decay)
    lowest = (log_decay - high.astype(F32) - low.astype(F32)).astype(BF16)
    cumul = dot(high, upper) + (dot(low, upper) + dot(lowest, upper))
    fade = jnp.exp(cumul)
    to_end = jnp.exp(cumul[:, rows - 1 : rows] - cumul)
    pad = jnp.zeros((128 - 4 * heads, rows), F32)
    cols = jnp.concatenate([cumul, strength, strength * fade, fade, pad], 0).T
    rows_out[...] = cumul
    cols_out[...] = cols

    line = lax.broadcasted_iota(jnp.int32, (HALF, HALF), 0)
    across = lax.broadcasted_iota(jnp.int32, (HALF, HALF), 1)
    below = line > across
    eye = jnp.where(line == across, 1.0, 0.0)
    parts = rows // HALF
    lowers = []
    rhs = []
    ends = []
    for key_head in range(key_heads):
        lanes = slice(key_head * KD, (key_head + 1) * KD)
        key = unit_rows(
            conv_rows(
                qk[1, :, lanes].astype(F32),
                hist_qk[1, :, lanes].astype(F32),
                conv_qk[1, :, lanes].astype(F32),
                first,
            )
        )
        key_low = key.astype(BF16)
        keys_out[key_head] = key_low
        dots = dot_nt(key_low, key_low)
        key_t = key.T
        for head in (2 * key_head, 2 * key_head + 1):
            lanes = slice(head * DV, (head + 1) * DV)
            val = conv_rows(
                value[:, lanes].astype(F32),
                hist_value[:, lanes].astype(F32),
                conv_value[:, lanes].astype(F32),
                first,
            )
            col = cols[:, head : head + 1]
            beta = cols[:, heads + head : heads + head + 1]
            beta_fade = cols[:, 2 * heads + head : 2 * heads + head + 1]
            lower = {}
            for i in range(parts):
                for j in range(i + 1):
                    a = slice(i * HALF, (i + 1) * HALF)
                    b = slice(j * HALF, (j + 1) * HALF)
                    spread = jnp.exp(jnp.minimum(col[a] - cumul[head : head + 1, b], 0.0))
                    entry = beta[a] * spread * dots[a, b]
                    lower[i, j] = jnp.where(below, entry, 0.0) if i == j else entry
            lowers.append(lower)
            rhs.append(jnp.concatenate([beta_fade * key, beta * val], 1))
            ends.append((key_t * to_end[head : head + 1]).astype(BF16))

    names = [(head, i) for head in range(heads) for i in range(parts)]
    tri = {}
    for head, i in names:
        near = (line // 2) == (across // 2)
        tri[head, i] = eye - jnp.where(near, lowers[head][i, i], 0.0)
    size = 2
    while size < HALF:
        mask = ((line // (2 * size)) == (across // (2 * size))) & ((line // size) != (across // size))
        low = {n: tri[n].astype(BF16) for n in names}
        inner = {
            (head, i): dot(jnp.where(mask, lowers[head][i, i], 0.0).astype(BF16), low[head, i]).astype(BF16)
            for head, i in names
        }
        tri = {n: tri[n] - dot(low[n], inner[n]) for n in names}
        size *= 2
    tri = {n: tri[n].astype(BF16) for n in names}
    solved = [[] for _ in range(heads)]
    for i in range(parts):
        for head in range(heads):
            need = rhs[head][i * HALF : (i + 1) * HALF]
            for j in range(i):
                need = need - fine_dot(lowers[head][i, j], solved[head][j])
            solved[head].append(dot(tri[head, i], need.astype(BF16)))
    half = heads // 2
    for head in range(heads):
        both = jnp.concatenate(solved[head], 0).astype(BF16)
        solved_out[head] = both
        ended = dot(ends[head], both)
        fade_end = fade[head : head + 1, rows - 1 : rows]
        own = jnp.concatenate([eye * fade_end - ended[:, :KD], ended[:, KD:]], 1).astype(BF16)
        maps_out[head] = own
    send_out[...] = maps_out[pl.ds((1 - bit) * half, half)]


def query_kernel(
    place, qk, keys, solved, cumul, cols, hist_qk, conv_qk, gate_z, gain,
    reads_out, local_out, gate_out,
):
    heads, rows = cumul.shape
    first = place[0] == 0
    line = lax.broadcasted_iota(jnp.int32, (rows, rows), 0)
    across = lax.broadcasted_iota(jnp.int32, (rows, rows), 1)
    within = line >= across
    for key_head in range(heads // 2):
        lanes = slice(key_head * KD, (key_head + 1) * KD)
        query = unit_rows(
            conv_rows(
                qk[0, :, lanes].astype(F32),
                hist_qk[0, :, lanes].astype(F32),
                conv_qk[0, :, lanes].astype(F32),
                first,
            )
        ) * (KD**-0.5)
        dots = dot_nt(query.astype(BF16), keys[key_head])
        for head in (2 * key_head, 2 * key_head + 1):
            col = cols[:, head : head + 1]
            fade = cols[:, 3 * heads + head : 3 * heads + head + 1]
            spread = jnp.exp(jnp.minimum(col - cumul[head : head + 1], 0.0))
            attend = jnp.where(within, spread * dots, 0.0).astype(BF16)
            part = dot(attend, solved[head])
            reads_out[head] = (fade * query - part[:, :KD]).astype(BF16)
            local_out[head] = part[:, KD:]
            lanes = slice(head * DV, (head + 1) * DV)
            gate_out[head] = silu(gate_z[:, lanes].astype(F32)) * gain[...]


def join(outer, inner):
    product = dot(outer[:, :KD], inner)
    return jnp.concatenate([product[:, :KD], product[:, KD:] + outer[:, KD:].astype(F32)], 1)


def act(outer, state):
    return dot(outer[:, :KD], state) + outer[:, KD:].astype(F32)


def pair_kernel(place, maps, received, total_out):
    bit = place[1]
    half = received.shape[0]
    for j in range(half):
        mine, other = maps[bit * half + j], received[j]
        low, high = jnp.where(bit == 1, other, mine), jnp.where(bit == 1, mine, other)
        total_out[j] = join(high, low).astype(BF16)


def level_kernel(level, last, *refs):
    if level == 1:
        place, total, received, state_in, total_out, prefix_out = refs
    else:
        place, total, received, prefix, state_in, total_out, prefix_out = refs
    bit = place[level + 1]
    half = total.shape[0]
    line = lax.broadcasted_iota(jnp.int32, (KD, KD + DV), 0)
    across = lax.broadcasted_iota(jnp.int32, (KD, KD + DV), 1)
    same = jnp.where(line == across, 1.0, 0.0).astype(BF16)
    for j in range(half):
        mine, other = total[j], received[j]
        low, high = jnp.where(bit == 1, other, mine), jnp.where(bit == 1, mine, other)
        if level == 1:
            prefix_out[j] = jnp.where(bit == 1, low, same)
        else:
            prefix_out[j] = jnp.where(bit == 1, join(prefix[j], low).astype(BF16), prefix[j])
        if last:
            state = state_in[place[1] * half + j].astype(BF16)
            total_out[j] = act(high, act(low, state).astype(BF16)).astype(BF16)
        else:
            total_out[j] = join(high, low).astype(BF16)


def enter_kernel(top, place, prefix, state_in, came, maps, received, mine_out, send_out):
    bit = place[1]
    half = prefix.shape[0]
    for j in range(half):
        start = jnp.where(place[top + 1] == 1, came[j], state_in[bit * half + j].astype(BF16))
        entering = act(prefix[j], start).astype(BF16)
        low = jnp.where(bit == 1, received[j], maps[bit * half + j])
        passed = act(low, entering).astype(BF16)
        mine_out[j] = jnp.where(bit == 1, passed, entering)
        send_out[j] = jnp.where(bit == 1, entering, passed)


def output_kernel(
    place, mine, came, reads, local_reads, gate, w_out, send_out, keep_out, states_out, normed,
):
    bit = place[1]
    core = place[0]
    half = mine.shape[0]
    heads = 2 * half
    blocks = send_out.shape[0]
    width = send_out.shape[2]
    for j in range(heads):
        if j < half:
            head, state = bit * half + j, mine[j]
        else:
            head, state = (1 - bit) * half + (j - half), came[j - half]
        states_out[head] = state
        out = local_reads[head] + dot(reads[head], state)
        scale = lax.rsqrt(jnp.mean(out * out, axis=-1, keepdims=True) + 1e-06)
        lanes = pl.ds(pl.multiple_of(head * DV, DV), DV)
        normed[:, lanes] = (out * scale * gate[head]).astype(BF16)
    for j in range(blocks):
        for side, ref in ((1 - core, send_out), (core, keep_out)):
            lanes = pl.ds(pl.multiple_of((2 * j + side) * width, width), width)
            ref[j] = dot(normed[...], w_out[:, lanes]).astype(BF16)


def merge_kernel(place, keep, came, send_out, keep_out):
    bit = place[0]
    blocks = send_out.shape[0]
    for j in range(blocks):
        away, home = 2 * j + 1 - bit, 2 * j + bit
        send_out[j] = (keep[away].astype(F32) + came[away].astype(F32)).astype(BF16)
        keep_out[j] = keep[home].astype(F32) + came[home].astype(F32)


def checkpoint_kernel(maps, states, out):
    for head in range(maps.shape[0]):
        out[0, head] = act(maps[head], states[head])


def swapped(value, axis, step):
    count = lax.axis_size(axis)
    return lax.ppermute(value, axis, [(i, i ^ step) for i in range(count)])


def local(
    hidden_in, w_qk, w_value, w_outgate, w_ba, conv_qk, conv_value, hist_qk, hist_value,
    a_log, dt_bias, beta_bias, state_in, norm_gain, w_out,
):
    rows, width = hidden_in.shape
    key_cols = w_qk.shape[2]
    heads = a_log.shape[0]
    half = heads // 2
    taps = conv_value.shape[0]
    n_seq = lax.axis_size("seq")
    n_head = lax.axis_size("head")
    levels = n_seq.bit_length() - 1
    seq = lax.axis_index("seq")
    col = lax.axis_index("head")
    place = jnp.stack([seq] + [(seq >> level) & 1 for level in range(levels)]).astype(jnp.int32)

    halo = lax.ppermute(
        hidden_in[rows - HALO :], "seq", [(i, (i + 1) % n_seq) for i in range(n_seq)]
    )
    joined = jnp.concatenate([halo, hidden_in], 0)
    qk = jnp.einsum("td,dce->cte", joined, w_qk, preferred_element_type=F32).astype(BF16)
    value = jnp.dot(joined, w_value, preferred_element_type=F32).astype(BF16)
    gates = jnp.einsum("td,dch->cht", hidden_in, w_ba, preferred_element_type=F32).astype(BF16)
    params = jnp.stack([a_log, dt_bias, beta_bias], 1)
    hist_qk = jnp.pad(jnp.moveaxis(hist_qk, 1, 0), ((0, 0), (HALO - taps + 1, 0), (0, 0)))
    hist_value = jnp.pad(hist_value, ((HALO - taps + 1, 0), (0, 0)))
    conv_qk = jnp.moveaxis(conv_qk, 1, 0)

    keys, solved, maps, send, cumul, cols = call(
        prepare_kernel,
        (
            shape((half, rows, KD), BF16),
            shape((heads, rows, KD + DV), BF16),
            shape((heads, KD, KD + DV), BF16),
            shape((half, KD, KD + DV), BF16),
            shape((heads, rows), F32),
            shape((rows, 128), F32),
        ),
        [SMEM] + [VMEM] * 8,
        10**10,
        4 << 20,
    )(place, qk, value, gates, hist_qk, hist_value, conv_qk, conv_value, params)

    received = swapped(send, "seq", 1)
    gate_z = jnp.dot(hidden_in, w_outgate, preferred_element_type=F32).astype(BF16)
    reads, local_reads, gate = call(
        query_kernel,
        (
            shape((heads, rows, KD), BF16),
            shape((heads, rows, DV), F32),
            shape((heads, rows, DV), F32),
        ),
        [SMEM] + [VMEM] * 9,
        4 * 10**9,
        6 << 20,
    )(place, qk, keys, solved, cumul, cols, hist_qk, conv_qk, gate_z, norm_gain.reshape(1, DV))

    map_shape = shape((half, KD, KD + DV), BF16)
    state_shape = shape((half, KD, DV), BF16)
    total = call(pair_kernel, map_shape, [SMEM, VMEM, VMEM], 10**8, 1 << 20)(place, maps, received)
    prefix = ()
    for level in range(1, levels - 1):
        other = swapped(total, "seq", 1 << level)
        last = level == levels - 2
        total, prefix = call(
            functools.partial(level_kernel, level, last),
            (state_shape if last else map_shape, map_shape),
            [SMEM] + [VMEM] * (3 if level == 1 else 4),
            10**8,
            1 << 20,
        )(place, total, other, *prefix, state_in)
        prefix = (prefix,)
    came = swapped(total, "seq", 1 << (levels - 1))
    mine, send_state = call(
        functools.partial(enter_kernel, levels - 1),
        (state_shape, state_shape),
        [SMEM] + [VMEM] * 5,
        10**8,
        1 << 20,
    )(place, prefix[0], state_in, came, maps, received)
    other_state = swapped(send_state, "seq", 1)

    out_width = w_out.shape[1] // n_head
    blocks = n_head // 2
    side = jnp.stack([col & 1, place[1]]).astype(jnp.int32)
    send_out, keep, states = call(
        output_kernel,
        (
            shape((blocks, rows, out_width), BF16),
            shape((blocks, rows, out_width), BF16),
            shape((heads, KD, DV), BF16),
        ),
        [SMEM] + [VMEM] * 6,
        10**9,
        8 << 20,
        [pltpu.VMEM((rows, heads * DV), BF16)],
    )(side, mine, other_state, reads, local_reads, gate, w_out)
    came_out = swapped(send_out, "head", 1)
    step = 2
    while step < n_head:
        blocks //= 2
        send_out, keep = call(
            merge_kernel,
            (shape((blocks, rows, out_width), BF16), shape((blocks, rows, out_width), F32)),
            [SMEM, VMEM, VMEM],
            10**6,
            2 << 20,
        )(((col // step) & 1).astype(jnp.int32).reshape(1), keep, came_out)
        came_out = swapped(send_out, "head", step)
        step *= 2
    checkpoint = call(
        checkpoint_kernel, shape((1, heads, KD, DV), F32), [VMEM, VMEM], 10**8, 2 << 20
    )(maps, states)
    mixed = (keep[0].astype(F32) + came_out[0].astype(F32)).astype(BF16)
    return (mixed, checkpoint)


def solution(mesh):
    return jax.shard_map(
        local,
        mesh=mesh,
        in_specs=(
            P("seq", None),
            P(None, None, "head"),
            P(None, "head"),
            P(None, "head"),
            P(None, None, "head"),
            P(None, None, "head"),
            P(None, "head"),
            P(None, None, "head"),
            P(None, "head"),
            P("head"),
            P("head"),
            P("head"),
            P("head", None, None),
            P(),
            P("head", None),
        ),
        out_specs=(P("seq", "head"), P("seq", "head", None, None)),
        check_vma=False,
    )
```

```python
import functools

import jax
import jax.numpy as jnp
from jax import lax
from jax.experimental import pallas as pl
from jax.experimental.pallas import tpu as pltpu
from jax.sharding import PartitionSpec as P

KD = 128
DV = 128
HALF = 128
HALO = 8
F32 = jnp.float32
BF16 = jnp.bfloat16
VMEM = pl.BlockSpec(memory_space=pltpu.VMEM)
SMEM = pl.BlockSpec(memory_space=pltpu.SMEM)


def dot(left, right):
    return jnp.dot(left, right, preferred_element_type=F32)


def dot_nt(left, right):
    return lax.dot_general(left, right, (((1,), (1,)), ((), ())), preferred_element_type=F32)


def split(values):
    high = values.astype(BF16)
    return high, (values - high.astype(F32)).astype(BF16)


def fine_dot(left, right):
    left_hi, left_lo = split(left)
    right_hi, right_lo = split(right)
    return dot(left_hi, right_hi) + (dot(left_hi, right_lo) + dot(left_lo, right_hi))


def silu(values):
    return values / (1.0 + jnp.exp(-values))


def unit_rows(values):
    return values * lax.rsqrt(jnp.sum(values * values, axis=-1, keepdims=True) + 1e-06)


def conv_rows(block, halo, history, weight, first):
    rows = block.shape[0]
    taps = weight.shape[0]
    start = HALO - (taps - 1)
    joined = jnp.concatenate([jnp.where(first, history, halo), block], 0)
    total = weight[0:1] * joined[start : start + rows]
    for tap in range(1, taps):
        total = total + weight[tap : tap + 1] * joined[start + tap : start + tap + rows]
    return silu(total)


def call(kernel, out_shape, in_specs, flops, moved, scratch=()):
    return pl.pallas_call(
        kernel,
        out_shape=out_shape,
        in_specs=in_specs,
        out_specs=jax.tree.map(lambda _: VMEM, out_shape),
        scratch_shapes=list(scratch),
        compiler_params=pltpu.CompilerParams(vmem_limit_bytes=12 << 20),
        cost_estimate=pl.CostEstimate(flops=flops, bytes_accessed=moved, transcendentals=0),
    )


def shape(dims, dtype):
    return jax.ShapeDtypeStruct(dims, dtype)


def lane_block(index, width):
    return pl.ds(pl.multiple_of(index * width, width), width)


def picked(flag, values):
    count = values.shape[0] // 2
    return jnp.where(flag == 1, values[count:], values[:count])


def scalar_column(ref, start, count):
    index = lax.broadcasted_iota(jnp.int32, (count, 1), 0)
    column = jnp.zeros((count, 1), F32)
    for i in range(count):
        column = jnp.where(index == i, ref[start + i], column)
    return column


def load_small(hist_qk, conv_qk, part, hist_s, conv_s):
    taps = conv_qk.shape[0]
    hist_s[HALO - taps + 1 :, :] = hist_qk[...].astype(F32)[:, part, :]
    conv_s[...] = conv_qk[...].astype(F32)[:, part, :]


def key_block(qk, halo, hist_s, conv_s, part, index, first):
    key_cols = qk.shape[2]
    lanes = lane_block(index, KD)
    halo_lanes = lane_block(part * (key_cols // KD) + index, KD)
    return unit_rows(
        conv_rows(
            qk[part, :, lanes].astype(F32),
            halo[:, halo_lanes].astype(F32),
            hist_s[:, lanes],
            conv_s[:, lanes],
            first,
        )
    )


def prepare_kernel(
    own, place, a_log, dt_bias, beta_bias, qk, value, gates, halo, hist_qk, hist_value,
    conv_qk, conv_value, keys_out, solved_out, maps_out, rows_out, cols_out,
    hist_s, conv_s, hist_v,
):
    heads = gates.shape[1] // 2
    rows = gates.shape[2]
    key_heads = heads // 2
    key_cols = qk.shape[2]
    taps = conv_value.shape[0]
    first = place[0] == 0
    side = place[1] if own else 1 - place[1]
    load_small(hist_qk, conv_qk, 1, hist_s, conv_s)
    hist_v[HALO - taps + 1 :, :] = hist_value[...].astype(F32)
    strength = jax.nn.sigmoid(
        picked(side, gates[0].astype(F32)) + scalar_column(beta_bias, side * heads, heads)
    )
    decay_in = picked(side, gates[1].astype(F32)) + scalar_column(dt_bias, side * heads, heads)
    soft = jnp.maximum(decay_in, 0.0) + jnp.log1p(jnp.exp(-jnp.abs(decay_in)))
    log_decay = -jnp.exp(scalar_column(a_log, side * heads, heads)) * soft
    line = lax.broadcasted_iota(jnp.int32, (rows, rows), 0)
    across = lax.broadcasted_iota(jnp.int32, (rows, rows), 1)
    upper = jnp.where(line <= across, 1.0, 0.0).astype(BF16)
    high, low = split(log_decay)
    lowest = (log_decay - high.astype(F32) - low.astype(F32)).astype(BF16)
    cumul = dot(high, upper) + (dot(low, upper) + dot(lowest, upper))
    fade = jnp.exp(cumul)
    to_end = jnp.exp(cumul[:, rows - 1 : rows] - cumul)
    pad = jnp.zeros((128 - 4 * heads, rows), F32)
    cols = jnp.concatenate([cumul, strength, strength * fade, fade, pad], 0).T
    rows_out[...] = cumul
    cols_out[...] = cols

    line = lax.broadcasted_iota(jnp.int32, (HALF, HALF), 0)
    across = lax.broadcasted_iota(jnp.int32, (HALF, HALF), 1)
    below = line > across
    eye = jnp.where(line == across, 1.0, 0.0)
    parts = rows // HALF
    lowers = []
    rhs = []
    ends = []
    for key_head in range(key_heads):
        key = key_block(qk, halo, hist_s, conv_s, 1, side * key_heads + key_head, first)
        key_low = key.astype(BF16)
        keys_out[key_head] = key_low
        dots = dot_nt(key_low, key_low)
        key_t = key.T
        for head in (2 * key_head, 2 * key_head + 1):
            index = side * heads + head
            lanes = lane_block(index, DV)
            val = conv_rows(
                value[:, lanes].astype(F32),
                halo[:, lane_block(2 * key_cols // DV + index, DV)].astype(F32),
                hist_v[:, lanes],
                conv_value[:, lanes].astype(F32),
                first,
            )
            col = cols[:, head : head + 1]
            beta = cols[:, heads + head : heads + head + 1]
            beta_fade = cols[:, 2 * heads + head : 2 * heads + head + 1]
            lower = {}
            for i in range(parts):
                for j in range(i + 1):
                    a = slice(i * HALF, (i + 1) * HALF)
                    b = slice(j * HALF, (j + 1) * HALF)
                    spread = jnp.exp(jnp.minimum(col[a] - cumul[head : head + 1, b], 0.0))
                    entry = beta[a] * spread * dots[a, b]
                    lower[i, j] = jnp.where(below, entry, 0.0) if i == j else entry
            lowers.append(lower)
            rhs.append(jnp.concatenate([beta_fade * key, beta * val], 1))
            ends.append((key_t * to_end[head : head + 1]).astype(BF16))

    names = [(head, i) for head in range(heads) for i in range(parts)]
    tri = {}
    for head, i in names:
        near = (line // 2) == (across // 2)
        tri[head, i] = eye - jnp.where(near, lowers[head][i, i], 0.0)
    size = 2
    while size < HALF:
        mask = ((line // (2 * size)) == (across // (2 * size))) & ((line // size) != (across // size))
        low = {n: tri[n].astype(BF16) for n in names}
        inner = {
            (head, i): dot(jnp.where(mask, lowers[head][i, i], 0.0).astype(BF16), low[head, i]).astype(BF16)
            for head, i in names
        }
        tri = {n: tri[n] - dot(low[n], inner[n]) for n in names}
        size *= 2
    tri = {n: tri[n].astype(BF16) for n in names}
    solved = [[] for _ in range(heads)]
    for i in range(parts):
        for head in range(heads):
            need = rhs[head][i * HALF : (i + 1) * HALF]
            for j in range(i):
                need = need - fine_dot(lowers[head][i, j], solved[head][j])
            solved[head].append(dot(tri[head, i], need.astype(BF16)))
    for head in range(heads):
        both = jnp.concatenate(solved[head], 0).astype(BF16)
        solved_out[head] = both
        ended = dot(ends[head], both)
        fade_end = fade[head : head + 1, rows - 1 : rows]
        own = jnp.concatenate([eye * fade_end - ended[:, :KD], ended[:, KD:]], 1).astype(BF16)
        maps_out[head] = own


def query_kernel(
    own, place, qk, halo, hist_qk, conv_qk, keys, solved, cumul, cols, gate_z, gain,
    reads_out, local_out, gate_out, hist_s, conv_s,
):
    heads, rows = cumul.shape
    key_heads = heads // 2
    first = place[0] == 0
    side = place[1] if own else 1 - place[1]
    load_small(hist_qk, conv_qk, 0, hist_s, conv_s)
    line = lax.broadcasted_iota(jnp.int32, (rows, rows), 0)
    across = lax.broadcasted_iota(jnp.int32, (rows, rows), 1)
    within = line >= across
    for key_head in range(key_heads):
        query = key_block(qk, halo, hist_s, conv_s, 0, side * key_heads + key_head, first)
        query = query * (KD**-0.5)
        dots = dot_nt(query.astype(BF16), keys[key_head])
        for head in (2 * key_head, 2 * key_head + 1):
            col = cols[:, head : head + 1]
            fade = cols[:, 3 * heads + head : 3 * heads + head + 1]
            spread = jnp.exp(jnp.minimum(col - cumul[head : head + 1], 0.0))
            attend = jnp.where(within, spread * dots, 0.0).astype(BF16)
            part = dot(attend, solved[head])
            reads_out[head] = (fade * query - part[:, :KD]).astype(BF16)
            local_out[head] = part[:, KD:]
            lanes = lane_block(side * heads + head, DV)
            gate_out[head] = silu(gate_z[:, lanes].astype(F32)) * gain[...]


def join(outer, inner):
    product = dot(outer[:, :KD], inner)
    return jnp.concatenate([product[:, :KD], product[:, KD:] + outer[:, KD:].astype(F32)], 1)


def act(outer, state):
    return dot(outer[:, :KD], state) + outer[:, KD:].astype(F32)


def pair_kernel(place, maps, received, total_out):
    bit = place[1]
    for j in range(received.shape[0]):
        mine, other = maps[j], received[j]
        low, high = jnp.where(bit == 1, other, mine), jnp.where(bit == 1, mine, other)
        total_out[j] = join(high, low).astype(BF16)


def level_kernel(level, last, *refs):
    if level == 1:
        place, total, received, state_in, total_out, prefix_out = refs
    else:
        place, total, received, prefix, state_in, total_out, prefix_out = refs
    bit = place[level + 1]
    half = total.shape[0]
    line = lax.broadcasted_iota(jnp.int32, (KD, KD + DV), 0)
    across = lax.broadcasted_iota(jnp.int32, (KD, KD + DV), 1)
    same = jnp.where(line == across, 1.0, 0.0).astype(BF16)
    for j in range(half):
        mine, other = total[j], received[j]
        low, high = jnp.where(bit == 1, other, mine), jnp.where(bit == 1, mine, other)
        if level == 1:
            prefix_out[j] = jnp.where(bit == 1, low, same)
        else:
            prefix_out[j] = jnp.where(bit == 1, join(prefix[j], low).astype(BF16), prefix[j])
        if last:
            state = state_in[place[1] * half + j].astype(BF16)
            total_out[j] = act(high, act(low, state).astype(BF16)).astype(BF16)
        else:
            total_out[j] = join(high, low).astype(BF16)


def enter_kernel(top, place, prefix, state_in, came, maps, received, mine_out, send_out):
    bit = place[1]
    half = prefix.shape[0]
    for j in range(half):
        start = jnp.where(place[top + 1] == 1, came[j], state_in[bit * half + j].astype(BF16))
        entering = act(prefix[j], start).astype(BF16)
        low = jnp.where(bit == 1, received[j], maps[j])
        passed = act(low, entering).astype(BF16)
        mine_out[j] = jnp.where(bit == 1, passed, entering)
        send_out[j] = jnp.where(bit == 1, entering, passed)


def normed_rows(local_part, reads, gate, state):
    out = local_part + dot(reads, state)
    scale = lax.rsqrt(jnp.mean(out * out, axis=-1, keepdims=True) + 1e-06)
    return (out * scale * gate).astype(BF16)


def project(side, mine_rows, other_rows, w_out, away, send_out, keep_out):
    core, bit, lift = side[0], side[1], side[2]
    depth = w_out.shape[0] // 2
    width = send_out.shape[2]
    for j in range(send_out.shape[0]):
        block = 2 * j + (1 - lift if away else lift)
        for member, ref in ((1 - core, send_out), (core, keep_out)):
            lanes = lane_block(2 * block + member, width)
            own = w_out[pl.ds(pl.multiple_of(bit * depth, depth), depth), lanes]
            other = w_out[pl.ds(pl.multiple_of((1 - bit) * depth, depth), depth), lanes]
            ref[j] = (dot(mine_rows[...], own) + dot(other_rows[...], other)).astype(BF16)


def normed_kernel(states, reads, local_reads, gate, normed_out):
    for j in range(states.shape[0]):
        normed_out[:, j * DV : (j + 1) * DV] = normed_rows(
            local_reads[j], reads[j], gate[j], states[j]
        )


def away_kernel(
    side, states, reads, local_reads, gate, mine_rows, w_out, other_rows, send_out, keep_out
):
    normed_kernel(states, reads, local_reads, gate, other_rows)
    project(side, mine_rows, other_rows, w_out, True, send_out, keep_out)


def home_kernel(
    side, mine_rows, other_rows, w_out, maps, states, away_maps, away_states,
    send_out, keep_out, checkpoint,
):
    project(side, mine_rows, other_rows, w_out, False, send_out, keep_out)
    bit = side[1]
    half = maps.shape[0]
    for j in range(half):
        checkpoint[0, bit * half + j] = act(maps[j], states[j])
        checkpoint[0, (1 - bit) * half + j] = act(away_maps[j], away_states[j])


def swapped(value, axis, step):
    count = lax.axis_size(axis)
    return lax.ppermute(value, axis, [(i, i ^ step) for i in range(count)])


def local(
    hidden_in, w_qk, w_value, w_outgate, w_ba, conv_qk, conv_value, hist_qk, hist_value,
    a_log, dt_bias, beta_bias, state_in, norm_gain, w_out,
):
    rows, width = hidden_in.shape
    key_cols = w_qk.shape[2]
    heads = a_log.shape[0]
    half = heads // 2
    taps = conv_value.shape[0]
    n_seq = lax.axis_size("seq")
    n_head = lax.axis_size("head")
    levels = n_seq.bit_length() - 1
    seq = lax.axis_index("seq")
    col = lax.axis_index("head")
    place = jnp.stack([seq] + [(seq >> level) & 1 for level in range(levels)]).astype(jnp.int32)

    qk = jnp.einsum("td,dce->cte", hidden_in, w_qk, preferred_element_type=F32).astype(BF16)
    value = jnp.dot(hidden_in, w_value, preferred_element_type=F32).astype(BF16)
    tail = rows - HALO
    ends = jnp.concatenate([qk[0, tail:], qk[1, tail:], value[tail:]], 1)
    halo = lax.ppermute(ends, "seq", [(i, (i + 1) % n_seq) for i in range(n_seq)])
    gates = jnp.einsum("td,dch->cht", hidden_in, w_ba, preferred_element_type=F32).astype(BF16)

    def prepare(own):
        return call(
            functools.partial(prepare_kernel, own),
            (
                shape((half // 2, rows, KD), BF16),
                shape((half, rows, KD + DV), BF16),
                shape((half, KD, KD + DV), BF16),
                shape((half, rows), F32),
                shape((rows, 128), F32),
            ),
            [SMEM] * 4 + [VMEM] * 8,
            4 * 10**9,
            4 << 20,
            [
                pltpu.VMEM((HALO, key_cols), F32),
                pltpu.VMEM((taps, key_cols), F32),
                pltpu.VMEM((HALO, heads * DV), F32),
            ],
        )(
            place, a_log, dt_bias, beta_bias, qk, value, gates, halo, hist_qk, hist_value,
            conv_qk, conv_value,
        )

    def query(own, prepared):
        keys, solved, _, cumul, cols = prepared
        return call(
            functools.partial(query_kernel, own),
            (
                shape((half, rows, KD), BF16),
                shape((half, rows, DV), F32),
                shape((half, rows, DV), F32),
            ),
            [SMEM] + [VMEM] * 10,
            2 * 10**9,
            4 << 20,
            [pltpu.VMEM((HALO, key_cols), F32), pltpu.VMEM((taps, key_cols), F32)],
        )(
            place, qk, halo, hist_qk, conv_qk, keys, solved, cumul, cols, gate_z,
            norm_gain.reshape(1, DV),
        )

    away = prepare(False)
    received = swapped(away[2], "seq", 1)
    own = prepare(True)
    received, own = lax.optimization_barrier((received, own))
    maps = own[2]
    map_shape = shape((half, KD, KD + DV), BF16)
    state_shape = shape((half, KD, DV), BF16)
    total = call(pair_kernel, map_shape, [SMEM, VMEM, VMEM], 10**8, 1 << 20)(place, maps, received)
    prefix = ()
    for level in range(1, levels - 1):
        other = swapped(total, "seq", 1 << level)
        last = level == levels - 2
        total, prefix = call(
            functools.partial(level_kernel, level, last),
            (state_shape if last else map_shape, map_shape),
            [SMEM] + [VMEM] * (3 if level == 1 else 4),
            10**8,
            1 << 20,
        )(place, total, other, *prefix, state_in)
        prefix = (prefix,)
    came = swapped(total, "seq", 1 << (levels - 1))
    later, _ = lax.optimization_barrier((hidden_in, total))
    gate_z = jnp.dot(later, w_outgate, preferred_element_type=F32).astype(BF16)
    own_reads = query(True, own)
    away_reads = query(False, away)
    came, own_reads, away_reads = lax.optimization_barrier((came, own_reads, away_reads))
    mine, send_state = call(
        functools.partial(enter_kernel, levels - 1),
        (state_shape, state_shape),
        [SMEM] + [VMEM] * 5,
        10**8,
        1 << 20,
    )(place, prefix[0], state_in, came, maps, received)
    other_state = swapped(send_state, "seq", 1)

    out_width = w_out.shape[1] // n_head
    blocks = n_head // 4
    side = jnp.stack([col & 1, place[1], (col >> 1) & 1]).astype(jnp.int32)
    part_shape = shape((blocks, rows, out_width), BF16)
    rows_shape = shape((rows, half * DV), BF16)
    own_rows = call(normed_kernel, rows_shape, [VMEM] * 4, 10**9, 4 << 20)(mine, *own_reads)
    other_rows, send_out, keep = call(
        away_kernel,
        (rows_shape, part_shape, part_shape),
        [SMEM] + [VMEM] * 6,
        10**9,
        4 << 20,
    )(side, other_state, *away_reads, own_rows, w_out)
    came_out = swapped(send_out, "head", 1)
    total_out = (keep.astype(F32) + came_out.astype(F32)).astype(BF16)
    total_out, other_rows = lax.optimization_barrier((total_out, other_rows))
    came_far = swapped(total_out, "head", 2)
    send_out, keep, checkpoint = call(
        home_kernel,
        (part_shape, part_shape, shape((1, heads, KD, DV), F32)),
        [SMEM] + [VMEM] * 7,
        10**9,
        4 << 20,
    )(side, own_rows, other_rows, w_out, maps, mine, away[2], other_state)
    came_out = swapped(send_out, "head", 1)
    mixed = keep.astype(F32) + came_out.astype(F32) + came_far.astype(F32)
    step = 4
    while step < n_head:
        here = (col // step) & 1
        blocks //= 2
        pairs = mixed.reshape(blocks, 2, rows, out_width)
        send_out = lax.dynamic_index_in_dim(pairs, 1 - here, 1, False).astype(BF16)
        mixed = lax.dynamic_index_in_dim(pairs, here, 1, False)
        mixed = mixed + swapped(send_out, "head", step).astype(F32)
        step *= 2
    return (mixed[0].astype(BF16), checkpoint)


def solution(mesh):
    return jax.shard_map(
        local,
        mesh=mesh,
        in_specs=(
            P("seq", None),
            P(None, None, "head"),
            P(None, "head"),
            P(None, "head"),
            P(None, None, "head"),
            P(None, None, "head"),
            P(None, "head"),
            P(None, None, "head"),
            P(None, "head"),
            P("head"),
            P("head"),
            P("head"),
            P("head", None, None),
            P(),
            P("head", None),
        ),
        out_specs=(P("seq", "head"), P("seq", "head", None, None)),
        check_vma=False,
    )
```

```python
import functools

import jax
import jax.numpy as jnp
from jax import lax
from jax.experimental import pallas as pl
from jax.experimental.pallas import tpu as pltpu
from jax.sharding import PartitionSpec as P

KD = 128
DV = 128
HALF = 128
HALO = 16
F32 = jnp.float32
BF16 = jnp.bfloat16
VMEM = pl.BlockSpec(memory_space=pltpu.VMEM)
SMEM = pl.BlockSpec(memory_space=pltpu.SMEM)


def dot(left, right):
    return jnp.dot(left, right, preferred_element_type=F32)


def dot_nt(left, right):
    return lax.dot_general(left, right, (((1,), (1,)), ((), ())), preferred_element_type=F32)


def split(values):
    high = values.astype(BF16)
    return high, (values - high.astype(F32)).astype(BF16)


def fine_dot(left, right):
    left_hi, left_lo = split(left)
    right_hi, right_lo = split(right)
    return dot(left_hi, right_hi) + (dot(left_hi, right_lo) + dot(left_lo, right_hi))


def silu(values):
    return values / (1.0 + jnp.exp(-values))


def unit_rows(values):
    return values * lax.rsqrt(jnp.sum(values * values, axis=-1, keepdims=True) + 1e-06)


def conv_rows(block, halo, weight):
    rows = block.shape[0]
    taps = weight.shape[0]
    start = HALO - (taps - 1)
    joined = jnp.concatenate([halo, block], 0)
    total = weight[0:1] * joined[start : start + rows]
    for tap in range(1, taps):
        total = total + weight[tap : tap + 1] * joined[start + tap : start + tap + rows]
    return silu(total)


def call(kernel, out_shape, in_specs, flops, moved, scratch=()):
    return pl.pallas_call(
        kernel,
        out_shape=out_shape,
        in_specs=in_specs,
        out_specs=jax.tree.map(lambda _: VMEM, out_shape),
        scratch_shapes=list(scratch),
        compiler_params=pltpu.CompilerParams(vmem_limit_bytes=12 << 20),
        cost_estimate=pl.CostEstimate(flops=flops, bytes_accessed=moved, transcendentals=0),
    )


def shape(dims, dtype):
    return jax.ShapeDtypeStruct(dims, dtype)


def lane_block(index, width):
    return pl.ds(pl.multiple_of(index * width, width), width)


def picked(flag, values):
    count = values.shape[0] // 2
    return jnp.where(flag == 1, values[count:], values[:count])


def scalar_column(ref, start, count):
    index = lax.broadcasted_iota(jnp.int32, (count, 1), 0)
    column = jnp.zeros((count, 1), F32)
    for i in range(count):
        column = jnp.where(index == i, ref[start + i], column)
    return column


def load_small(hist_qk, conv_qk, part, hist_s, conv_s):
    taps = conv_qk.shape[0]
    if hist_s is not None:
        hist_s[HALO - taps + 1 :, :] = hist_qk[...].astype(F32)[:, part, :]
    conv_s[...] = conv_qk[...].astype(F32)[:, part, :]


def front_rows(block, halo, hist, weight, lanes, halo_lanes, first):
    before = jnp.where(first, hist[:, lanes], halo[:, halo_lanes].astype(F32))
    return conv_rows(block.astype(F32), before, weight)


def running(column, count):
    sums = [column[0:1]]
    for i in range(1, count):
        sums.append(sums[-1] + column[i : i + 1])
    return sums


def stacked(rows_in, width):
    return jnp.concatenate(rows_in + [jnp.zeros((HALO - len(rows_in), width), F32)], 0)


def prepare_kernel(
    own, place, a_log, dt_bias, beta_bias, qk, value, gates, conv_qk, conv_value,
    keys_out, solved_out, maps_out, rows_out, cols_out, conv_s,
):
    heads = gates.shape[1] // 2
    rows = gates.shape[2]
    key_heads = heads // 2
    taps = conv_value.shape[0]
    side = place[1] if own else 1 - place[1]
    load_small(None, conv_qk, 1, None, conv_s)
    zero = jnp.zeros((HALO, KD), F32)
    rest = lax.broadcasted_iota(jnp.int32, (heads, rows), 1) >= taps - 1
    strength = jax.nn.sigmoid(
        picked(side, gates[0].astype(F32)) + scalar_column(beta_bias, side * heads, heads)
    )
    decay_in = picked(side, gates[1].astype(F32)) + scalar_column(dt_bias, side * heads, heads)
    soft = jnp.maximum(decay_in, 0.0) + jnp.log1p(jnp.exp(-jnp.abs(decay_in)))
    log_decay = -jnp.exp(scalar_column(a_log, side * heads, heads)) * soft
    raw = [strength, log_decay]
    strength = jnp.where(rest, strength, 0.0)
    log_decay = jnp.where(rest, log_decay, 0.0)
    line = lax.broadcasted_iota(jnp.int32, (rows, rows), 0)
    across = lax.broadcasted_iota(jnp.int32, (rows, rows), 1)
    upper = jnp.where(line <= across, 1.0, 0.0).astype(BF16)
    high, low = split(log_decay)
    lowest = (log_decay - high.astype(F32) - low.astype(F32)).astype(BF16)
    cumul = dot(high, upper) + (dot(low, upper) + dot(lowest, upper))
    fade = jnp.exp(cumul)
    to_end = jnp.exp(cumul[:, rows - 1 : rows] - cumul)
    pad = jnp.zeros((128 - 6 * heads, rows), F32)
    cols = jnp.concatenate([cumul, strength, strength * fade, fade, *raw, pad], 0).T
    rows_out[...] = cumul
    cols_out[...] = cols

    line = lax.broadcasted_iota(jnp.int32, (HALF, HALF), 0)
    across = lax.broadcasted_iota(jnp.int32, (HALF, HALF), 1)
    below = line > across
    eye = jnp.where(line == across, 1.0, 0.0)
    parts = rows // HALF
    lowers = []
    rhs = []
    ends = []
    for key_head in range(key_heads):
        lanes = lane_block(side * key_heads + key_head, KD)
        key = unit_rows(conv_rows(qk[1, :, lanes].astype(F32), zero, conv_s[:, lanes]))
        key_low = key.astype(BF16)
        keys_out[key_head] = key_low
        dots = dot_nt(key_low, key_low)
        key_t = key.T
        for head in (2 * key_head, 2 * key_head + 1):
            index = side * heads + head
            lanes = lane_block(index, DV)
            val = conv_rows(value[:, lanes].astype(F32), zero, conv_value[:, lanes].astype(F32))
            col = cols[:, head : head + 1]
            beta = cols[:, heads + head : heads + head + 1]
            beta_fade = cols[:, 2 * heads + head : 2 * heads + head + 1]
            lower = {}
            for i in range(parts):
                for j in range(i + 1):
                    a = slice(i * HALF, (i + 1) * HALF)
                    b = slice(j * HALF, (j + 1) * HALF)
                    spread = jnp.exp(jnp.minimum(col[a] - cumul[head : head + 1, b], 0.0))
                    entry = beta[a] * spread * dots[a, b]
                    lower[i, j] = jnp.where(below, entry, 0.0) if i == j else entry
            lowers.append(lower)
            rhs.append(jnp.concatenate([beta_fade * key, beta * val], 1))
            ends.append((key_t * to_end[head : head + 1]).astype(BF16))

    names = [(head, i) for head in range(heads) for i in range(parts)]
    tri = {}
    for head, i in names:
        near = (line // 2) == (across // 2)
        tri[head, i] = eye - jnp.where(near, lowers[head][i, i], 0.0)
    size = 2
    while size < HALF:
        mask = ((line // (2 * size)) == (across // (2 * size))) & ((line // size) != (across // size))
        low = {n: tri[n].astype(BF16) for n in names}
        inner = {
            (head, i): dot(jnp.where(mask, lowers[head][i, i], 0.0).astype(BF16), low[head, i]).astype(BF16)
            for head, i in names
        }
        tri = {n: tri[n] - dot(low[n], inner[n]) for n in names}
        size *= 2
    tri = {n: tri[n].astype(BF16) for n in names}
    solved = [[] for _ in range(heads)]
    for i in range(parts):
        for head in range(heads):
            need = rhs[head][i * HALF : (i + 1) * HALF]
            for j in range(i):
                need = need - fine_dot(lowers[head][i, j], solved[head][j])
            solved[head].append(dot(tri[head, i], need.astype(BF16)))
    for head in range(heads):
        both = jnp.concatenate(solved[head], 0).astype(BF16)
        solved_out[head] = both
        ended = dot(ends[head], both)
        fade_end = fade[head : head + 1, rows - 1 : rows]
        own = jnp.concatenate([eye * fade_end - ended[:, :KD], ended[:, KD:]], 1)
        maps_out[head] = own


def front_kernel(
    own, place, qk, value, halo, hist_qk, hist_value, conv_qk, conv_value, rest, cols,
    maps_out, keys_out, solved_out, hist_s, conv_s, hist_v,
):
    heads = rest.shape[0]
    key_heads = heads // 2
    key_cols = qk.shape[2]
    taps = conv_value.shape[0]
    count = taps - 1
    first = place[0] == 0
    side = place[1] if own else 1 - place[1]
    load_small(hist_qk, conv_qk, 1, hist_s, conv_s)
    hist_v[HALO - count :, :] = hist_value[...].astype(F32)
    for pair in range(key_heads):
        index = side * key_heads + pair
        lanes = lane_block(index, KD)
        key = unit_rows(
            front_rows(
                qk[1, :HALO, lanes], halo, hist_s, conv_s[:, lanes], lanes,
                lane_block(key_cols // KD + index, KD), first,
            )
        )
        keys = [key[i : i + 1] for i in range(count)]
        keys_out[pair] = stacked(keys, KD)
        dots = {
            (i, j): jnp.sum(keys[i] * keys[j], axis=-1, keepdims=True)
            for i in range(count)
            for j in range(i)
        }
        for head in (2 * pair, 2 * pair + 1):
            index = side * heads + head
            lanes = lane_block(index, DV)
            val = front_rows(
                value[:HALO, lanes], halo, hist_v, conv_value[:, lanes].astype(F32), lanes,
                lane_block(2 * key_cols // DV + index, DV), first,
            )
            beta = cols[:HALO, 4 * heads + head : 4 * heads + head + 1]
            cumul = running(cols[:HALO, 5 * heads + head : 5 * heads + head + 1], count)
            solved = []
            for i in range(count):
                need = jnp.concatenate([jnp.exp(cumul[i]) * keys[i], val[i : i + 1]], 1)
                for j in range(i):
                    need = need - (jnp.exp(cumul[i] - cumul[j]) * dots[i, j]) * solved[j]
                solved.append(beta[i : i + 1] * need)
            solved_out[head] = stacked(solved, KD + DV)
            ends = stacked([jnp.exp(cumul[-1] - cumul[i]) * keys[i] for i in range(count)], KD)
            maps_out[head] = put_ahead(rest[head], jnp.exp(cumul[-1]), ends, solved_out[head]).astype(BF16)


def put_ahead(rest, fade, ends, solved):
    through = dot_nt(rest[:, :KD].astype(BF16), ends.astype(BF16)).astype(BF16)
    moved = dot(through, solved.astype(BF16))
    return jnp.concatenate([fade * rest[:, :KD] - moved[:, :KD], rest[:, KD:] + moved[:, KD:]], 1)


def query_kernel(
    own, place, qk, halo, hist_qk, conv_qk, keys, solved, cumul, cols, front_keys, front_solved,
    gate_z, gain, reads_out, local_out, gate_out, hist_s, conv_s,
):
    heads, rows = cumul.shape
    key_heads = heads // 2
    count = conv_qk.shape[0] - 1
    first = place[0] == 0
    side = place[1] if own else 1 - place[1]
    load_small(hist_qk, conv_qk, 0, hist_s, conv_s)
    line = lax.broadcasted_iota(jnp.int32, (rows, rows), 0)
    across = lax.broadcasted_iota(jnp.int32, (rows, rows), 1)
    within = line >= across
    in_front = lax.broadcasted_iota(jnp.int32, (HALO, 1), 0) < count
    zero = jnp.zeros((HALO, KD), F32)
    for pair in range(key_heads):
        lanes = lane_block(side * key_heads + pair, KD)
        query = unit_rows(conv_rows(qk[0, :, lanes].astype(F32), zero, conv_s[:, lanes]))
        query = query * (KD**-0.5)
        ahead = unit_rows(
            front_rows(qk[0, :HALO, lanes], halo, hist_s, conv_s[:, lanes], lanes, lanes, first)
        ) * (KD**-0.5)
        dots = dot_nt(query.astype(BF16), keys[pair])
        front = [front_keys[pair, i : i + 1] for i in range(count)]
        for head in (2 * pair, 2 * pair + 1):
            col = cols[:, head : head + 1]
            fade = cols[:, 3 * heads + head : 3 * heads + head + 1]
            spread = jnp.exp(jnp.minimum(col - cumul[head : head + 1], 0.0))
            attend = jnp.where(within, spread * dots, 0.0).astype(BF16)
            part = dot(attend, solved[head])
            reads = jnp.concatenate([fade * query - part[:, :KD], part[:, KD:]], 1)
            sums = running(cols[:HALO, 5 * heads + head : 5 * heads + head + 1], count)
            ends = stacked([jnp.exp(sums[-1] - sums[i]) * front[i] for i in range(count)], KD)
            reads = put_ahead(reads, jnp.exp(sums[-1]), ends, front_solved[head])
            first_rows = []
            for i in range(count):
                asked = ahead[i : i + 1]
                row = jnp.concatenate([jnp.exp(sums[i]) * asked, jnp.zeros((1, DV), F32)], 1)
                for j in range(i + 1):
                    weight = jnp.exp(sums[i] - sums[j]) * jnp.sum(
                        asked * front[j], axis=-1, keepdims=True
                    )
                    term = weight * front_solved[head, j : j + 1]
                    row = row + jnp.concatenate([-term[:, :KD], term[:, KD:]], 1)
                first_rows.append(row)
            top = jnp.where(in_front, stacked(first_rows, KD + DV), reads[:HALO])
            reads = jnp.concatenate([top, reads[HALO:]], 0)
            reads_out[head] = reads[:, :KD].astype(BF16)
            local_out[head] = reads[:, KD:]
            lanes = lane_block(side * heads + head, DV)
            gate_out[head] = silu(gate_z[:, lanes].astype(F32)) * gain[...]


def join(outer, inner):
    product = dot(outer[:, :KD], inner)
    return jnp.concatenate([product[:, :KD], product[:, KD:] + outer[:, KD:].astype(F32)], 1)


def act(outer, state):
    return dot(outer[:, :KD], state) + outer[:, KD:].astype(F32)


def pair_kernel(place, maps, received, total_out):
    bit = place[1]
    for j in range(received.shape[0]):
        mine, other = maps[j], received[j]
        low, high = jnp.where(bit == 1, other, mine), jnp.where(bit == 1, mine, other)
        total_out[j] = join(high, low).astype(BF16)


def level_kernel(level, last, *refs):
    if level == 1:
        place, total, received, state_in, total_out, prefix_out = refs
    else:
        place, total, received, prefix, state_in, total_out, prefix_out = refs
    bit = place[level + 1]
    half = total.shape[0]
    line = lax.broadcasted_iota(jnp.int32, (KD, KD + DV), 0)
    across = lax.broadcasted_iota(jnp.int32, (KD, KD + DV), 1)
    same = jnp.where(line == across, 1.0, 0.0).astype(BF16)
    for j in range(half):
        mine, other = total[j], received[j]
        low, high = jnp.where(bit == 1, other, mine), jnp.where(bit == 1, mine, other)
        if level == 1:
            prefix_out[j] = jnp.where(bit == 1, low, same)
        else:
            prefix_out[j] = jnp.where(bit == 1, join(prefix[j], low).astype(BF16), prefix[j])
        if last:
            state = state_in[place[1] * half + j].astype(BF16)
            total_out[j] = act(high, act(low, state).astype(BF16)).astype(BF16)
        else:
            total_out[j] = join(high, low).astype(BF16)


def enter_kernel(top, place, prefix, state_in, came, maps, received, mine_out, send_out):
    bit = place[1]
    half = prefix.shape[0]
    for j in range(half):
        start = jnp.where(place[top + 1] == 1, came[j], state_in[bit * half + j].astype(BF16))
        entering = act(prefix[j], start).astype(BF16)
        low = jnp.where(bit == 1, received[j], maps[j])
        passed = act(low, entering).astype(BF16)
        mine_out[j] = jnp.where(bit == 1, passed, entering)
        send_out[j] = jnp.where(bit == 1, entering, passed)


def normed_rows(local_part, reads, gate, state):
    out = local_part + dot(reads, state)
    scale = lax.rsqrt(jnp.mean(out * out, axis=-1, keepdims=True) + 1e-06)
    return (out * scale * gate).astype(BF16)


def project(side, mine_rows, other_rows, w_out, away, send_out, keep_out):
    core, bit, lift = side[0], side[1], side[2]
    depth = w_out.shape[0] // 2
    width = send_out.shape[2]
    for j in range(send_out.shape[0]):
        block = 2 * j + (1 - lift if away else lift)
        for member, ref in ((1 - core, send_out), (core, keep_out)):
            lanes = lane_block(2 * block + member, width)
            own = w_out[pl.ds(pl.multiple_of(bit * depth, depth), depth), lanes]
            other = w_out[pl.ds(pl.multiple_of((1 - bit) * depth, depth), depth), lanes]
            ref[j] = (dot(mine_rows[...], own) + dot(other_rows[...], other)).astype(BF16)


def normed_kernel(states, reads, local_reads, gate, normed_out):
    for j in range(states.shape[0]):
        normed_out[:, j * DV : (j + 1) * DV] = normed_rows(
            local_reads[j], reads[j], gate[j], states[j]
        )


def away_kernel(
    side, states, reads, local_reads, gate, mine_rows, w_out, other_rows, send_out, keep_out
):
    normed_kernel(states, reads, local_reads, gate, other_rows)
    project(side, mine_rows, other_rows, w_out, True, send_out, keep_out)


def home_kernel(
    side, mine_rows, other_rows, w_out, maps, states, away_maps, away_states,
    send_out, keep_out, checkpoint,
):
    project(side, mine_rows, other_rows, w_out, False, send_out, keep_out)
    bit = side[1]
    half = maps.shape[0]
    for j in range(half):
        checkpoint[0, bit * half + j] = act(maps[j], states[j])
        checkpoint[0, (1 - bit) * half + j] = act(away_maps[j], away_states[j])


def swapped(value, axis, step):
    count = lax.axis_size(axis)
    return lax.ppermute(value, axis, [(i, i ^ step) for i in range(count)])


def local(
    hidden_in, w_qk, w_value, w_outgate, w_ba, conv_qk, conv_value, hist_qk, hist_value,
    a_log, dt_bias, beta_bias, state_in, norm_gain, w_out,
):
    rows, width = hidden_in.shape
    key_cols = w_qk.shape[2]
    heads = a_log.shape[0]
    half = heads // 2
    taps = conv_value.shape[0]
    n_seq = lax.axis_size("seq")
    n_head = lax.axis_size("head")
    levels = n_seq.bit_length() - 1
    seq = lax.axis_index("seq")
    col = lax.axis_index("head")
    place = jnp.stack([seq] + [(seq >> level) & 1 for level in range(levels)]).astype(jnp.int32)

    qk = jnp.einsum("td,dce->cte", hidden_in, w_qk, preferred_element_type=F32).astype(BF16)
    value = jnp.dot(hidden_in, w_value, preferred_element_type=F32).astype(BF16)
    tail = rows - HALO
    ends = jnp.concatenate([qk[0, tail:], qk[1, tail:], value[tail:]], 1)
    halo = lax.ppermute(ends, "seq", [(i, (i + 1) % n_seq) for i in range(n_seq)])
    gates = jnp.einsum("td,dch->cht", hidden_in, w_ba, preferred_element_type=F32).astype(BF16)

    small = [pltpu.VMEM((HALO, key_cols), F32), pltpu.VMEM((taps, key_cols), F32)]

    def prepare(own, qk):
        return call(
            functools.partial(prepare_kernel, own),
            (
                shape((half // 2, rows, KD), BF16),
                shape((half, rows, KD + DV), BF16),
                shape((half, KD, KD + DV), F32),
                shape((half, rows), F32),
                shape((rows, 128), F32),
            ),
            [SMEM] * 4 + [VMEM] * 5,
            4 * 10**9,
            4 << 20,
            small[1:],
        )(place, a_log, dt_bias, beta_bias, qk, value, gates, conv_qk, conv_value)

    def front(own, prepared):
        return call(
            functools.partial(front_kernel, own),
            (
                shape((half, KD, KD + DV), BF16),
                shape((half // 2, HALO, KD), F32),
                shape((half, HALO, KD + DV), F32),
            ),
            [SMEM] + [VMEM] * 9,
            10**8,
            1 << 20,
            small + [pltpu.VMEM((HALO, heads * DV), F32)],
        )(
            place, qk, value, halo, hist_qk, hist_value, conv_qk, conv_value,
            prepared[2], prepared[4],
        )

    def query(own, prepared, fronted, qk):
        keys, solved, _, cumul, cols = prepared
        return call(
            functools.partial(query_kernel, own),
            (
                shape((half, rows, KD), BF16),
                shape((half, rows, DV), F32),
                shape((half, rows, DV), F32),
            ),
            [SMEM] + [VMEM] * 12,
            2 * 10**9,
            4 << 20,
            small,
        )(
            place, qk, halo, hist_qk, conv_qk, keys, solved, cumul, cols, fronted[1], fronted[2],
            gate_z, norm_gain.reshape(1, DV),
        )

    away = prepare(False, qk)
    halo, away = lax.optimization_barrier((halo, away))
    away_front = front(False, away)
    received = swapped(away_front[0], "seq", 1)
    later, _ = lax.optimization_barrier((qk, away_front[0]))
    own = prepare(True, later)
    own_front = front(True, own)
    maps, away_maps = own_front[0], away_front[0]
    received, own, maps = lax.optimization_barrier((received, own, maps))

    map_shape = shape((half, KD, KD + DV), BF16)
    state_shape = shape((half, KD, DV), BF16)
    total = call(pair_kernel, map_shape, [SMEM, VMEM, VMEM], 10**8, 1 << 20)(place, maps, received)
    prefix = ()
    for level in range(1, levels - 1):
        other = swapped(total, "seq", 1 << level)
        if level == 1:
            later, _ = lax.optimization_barrier((hidden_in, total))
            gate_z = jnp.dot(later, w_outgate, preferred_element_type=F32).astype(BF16)
            other, gate_z = lax.optimization_barrier((other, gate_z))
        last = level == levels - 2
        total, prefix = call(
            functools.partial(level_kernel, level, last),
            (state_shape if last else map_shape, map_shape),
            [SMEM] + [VMEM] * (3 if level == 1 else 4),
            10**8,
            1 << 20,
        )(place, total, other, *prefix, state_in)
        prefix = (prefix,)
    came = swapped(total, "seq", 1 << (levels - 1))
    later, _ = lax.optimization_barrier((qk, total))
    own_reads = query(True, own, own_front, later)
    away_reads = query(False, away, away_front, later)
    came, own_reads, away_reads = lax.optimization_barrier((came, own_reads, away_reads))
    mine, send_state = call(
        functools.partial(enter_kernel, levels - 1),
        (state_shape, state_shape),
        [SMEM] + [VMEM] * 5,
        10**8,
        1 << 20,
    )(place, prefix[0], state_in, came, maps, received)
    other_state = swapped(send_state, "seq", 1)

    out_width = w_out.shape[1] // n_head
    blocks = n_head // 4
    side = jnp.stack([col & 1, place[1], (col >> 1) & 1]).astype(jnp.int32)
    part_shape = shape((blocks, rows, out_width), BF16)
    rows_shape = shape((rows, half * DV), BF16)
    own_rows = call(normed_kernel, rows_shape, [VMEM] * 4, 10**9, 4 << 20)(mine, *own_reads)
    other_rows, send_out, keep = call(
        away_kernel,
        (rows_shape, part_shape, part_shape),
        [SMEM] + [VMEM] * 6,
        10**9,
        4 << 20,
    )(side, other_state, *away_reads, own_rows, w_out)
    came_out = swapped(send_out, "head", 1)
    total_out = (keep.astype(F32) + came_out.astype(F32)).astype(BF16)
    total_out, other_rows = lax.optimization_barrier((total_out, other_rows))
    came_far = swapped(total_out, "head", 2)
    send_out, keep, checkpoint = call(
        home_kernel,
        (part_shape, part_shape, shape((1, heads, KD, DV), F32)),
        [SMEM] + [VMEM] * 7,
        10**9,
        4 << 20,
    )(side, own_rows, other_rows, w_out, maps, mine, away_maps, other_state)
    came_out = swapped(send_out, "head", 1)
    mixed = keep.astype(F32) + came_out.astype(F32) + came_far.astype(F32)
    step = 4
    while step < n_head:
        here = (col // step) & 1
        blocks //= 2
        pairs = mixed.reshape(blocks, 2, rows, out_width)
        send_out = lax.dynamic_index_in_dim(pairs, 1 - here, 1, False).astype(BF16)
        mixed = lax.dynamic_index_in_dim(pairs, here, 1, False)
        mixed = mixed + swapped(send_out, "head", step).astype(F32)
        step *= 2
    return (mixed[0].astype(BF16), checkpoint)


def solution(mesh):
    return jax.shard_map(
        local,
        mesh=mesh,
        in_specs=(
            P("seq", None),
            P(None, None, "head"),
            P(None, "head"),
            P(None, "head"),
            P(None, None, "head"),
            P(None, None, "head"),
            P(None, "head"),
            P(None, None, "head"),
            P(None, "head"),
            P("head"),
            P("head"),
            P("head"),
            P("head", None, None),
            P(),
            P("head", None),
        ),
        out_specs=(P("seq", "head"), P("seq", "head", None, None)),
        check_vma=False,
    )
```

```python
import functools

import jax
import jax.numpy as jnp
from jax import lax
from jax.experimental import pallas as pl
from jax.experimental.pallas import tpu as pltpu
from jax.sharding import PartitionSpec as P

KD = 128
DV = 128
HALF = 128
HALO = 16
TAIL = 8
F32 = jnp.float32
BF16 = jnp.bfloat16
VMEM = pl.BlockSpec(memory_space=pltpu.VMEM)
SMEM = pl.BlockSpec(memory_space=pltpu.SMEM)


def dot(left, right):
    return jnp.dot(left, right, preferred_element_type=F32)


def dot_nt(left, right):
    return lax.dot_general(left, right, (((1,), (1,)), ((), ())), preferred_element_type=F32)


def split(values):
    high = values.astype(BF16)
    return high, (values - high.astype(F32)).astype(BF16)


def fine_dot(left, right):
    left_hi, left_lo = split(left)
    right_hi, right_lo = split(right)
    return dot(left_hi, right_hi) + (dot(left_hi, right_lo) + dot(left_lo, right_hi))


def silu(values):
    return values / (1.0 + jnp.exp(-values))


def unit_rows(values):
    return values * lax.rsqrt(jnp.sum(values * values, axis=-1, keepdims=True) + 1e-06)


def conv_rows(block, halo, weight):
    rows = block.shape[0]
    taps = weight.shape[0]
    start = HALO - (taps - 1)
    joined = jnp.concatenate([halo, block], 0)
    total = weight[0:1] * joined[start : start + rows]
    for tap in range(1, taps):
        total = total + weight[tap : tap + 1] * joined[start + tap : start + tap + rows]
    return silu(total)


class Flags:
    def __init__(self, names, refs):
        self.refs = dict(zip(names, refs))

    def __getitem__(self, name):
        return self.refs[name][0]


def call(kernel, out_shape, in_specs, flops, moved, scratch=(), flags=None):
    names = tuple(flags or ())

    def body(*refs):
        if names:
            kernel(Flags(names, refs[: len(names)]), *refs[len(names) :])
        else:
            kernel(*refs)

    run = pl.pallas_call(
        body,
        out_shape=out_shape,
        in_specs=[SMEM] * len(names) + in_specs,
        out_specs=jax.tree.map(lambda _: VMEM, out_shape),
        scratch_shapes=list(scratch),
        compiler_params=pltpu.CompilerParams(vmem_limit_bytes=12 << 20),
        cost_estimate=pl.CostEstimate(flops=6 * flops, bytes_accessed=6 * moved, transcendentals=0),
    )
    return lambda *args: run(*[flags[name] for name in names], *args)


def shape(dims, dtype):
    return jax.ShapeDtypeStruct(dims, dtype)


def lane_block(index, width):
    return pl.ds(pl.multiple_of(index * width, width), width)


def picked(flag, values):
    count = values.shape[0] // 2
    return jnp.where(flag == 1, values[count:], values[:count])


def as_column(row):
    count = row.shape[1]
    line = lax.broadcasted_iota(jnp.int32, (count, count), 0)
    across = lax.broadcasted_iota(jnp.int32, (count, count), 1)
    return jnp.sum(jnp.where(line == across, row, 0.0), axis=1, keepdims=True)


def load_small(hist_qk, conv_qk, part, hist_s, conv_s):
    taps = conv_qk.shape[0]
    if hist_s is not None:
        hist_s[HALO - taps + 1 :, :] = hist_qk[...].astype(F32)[:, part, :]
    conv_s[...] = conv_qk[...].astype(F32)[:, part, :]


def front_rows(block, halo, hist, weight, lanes, halo_lanes, first):
    before = jnp.where(first, hist[HALO - TAIL :, lanes], halo[:, halo_lanes].astype(F32))
    pad = jnp.zeros((HALO - TAIL, before.shape[1]), F32)
    return conv_rows(block.astype(F32), jnp.concatenate([pad, before], 0), weight)


def running(column, count):
    sums = [column[0:1]]
    for i in range(1, count):
        sums.append(sums[-1] + column[i : i + 1])
    return sums


def stacked(rows_in, width):
    return jnp.concatenate(rows_in + [jnp.zeros((HALO - len(rows_in), width), F32)], 0)


def prepare_kernel(
    own, place, a_log, dt_bias, beta_bias, qk, value, gates, conv_qk, conv_value,
    keys_out, solved_out, maps_out, rows_out, cols_out, conv_s,
):
    heads = gates.shape[1] // 2
    rows = gates.shape[2]
    key_heads = heads // 2
    taps = conv_value.shape[0]
    side = place[1] if own else 1 - place[1]
    load_small(None, conv_qk, 1, None, conv_s)
    zero = jnp.zeros((HALO, KD), F32)
    rest = lax.broadcasted_iota(jnp.int32, (heads, rows), 1) >= taps - 1
    strength = jax.nn.sigmoid(
        picked(side, gates[0].astype(F32)) + picked(side, as_column(beta_bias[...]))
    )
    decay_in = picked(side, gates[1].astype(F32)) + picked(side, as_column(dt_bias[...]))
    soft = jnp.maximum(decay_in, 0.0) + jnp.log1p(jnp.exp(-jnp.abs(decay_in)))
    log_decay = -jnp.exp(picked(side, as_column(a_log[...]))) * soft
    raw = [strength, log_decay]
    strength = jnp.where(rest, strength, 0.0)
    log_decay = jnp.where(rest, log_decay, 0.0)
    line = lax.broadcasted_iota(jnp.int32, (rows, rows), 0)
    across = lax.broadcasted_iota(jnp.int32, (rows, rows), 1)
    upper = jnp.where(line <= across, 1.0, 0.0).astype(BF16)
    high, low = split(log_decay)
    lowest = (log_decay - high.astype(F32) - low.astype(F32)).astype(BF16)
    cumul = dot(high, upper) + (dot(low, upper) + dot(lowest, upper))
    fade = jnp.exp(cumul)
    to_end = jnp.exp(cumul[:, rows - 1 : rows] - cumul)
    pad = jnp.zeros((128 - 6 * heads, rows), F32)
    cols = jnp.concatenate([cumul, strength, strength * fade, fade, *raw, pad], 0).T
    rows_out[...] = cumul
    cols_out[...] = cols

    line = lax.broadcasted_iota(jnp.int32, (HALF, HALF), 0)
    across = lax.broadcasted_iota(jnp.int32, (HALF, HALF), 1)
    below = line > across
    eye = jnp.where(line == across, 1.0, 0.0)
    parts = rows // HALF
    lowers = []
    rhs = []
    ends = []
    for key_head in range(key_heads):
        lanes = lane_block(side * key_heads + key_head, KD)
        key = unit_rows(conv_rows(qk[1, :, lanes].astype(F32), zero, conv_s[:, lanes]))
        key_low = key.astype(BF16)
        keys_out[key_head] = key_low
        dots = dot_nt(key_low, key_low)
        key_t = key.T
        for head in (2 * key_head, 2 * key_head + 1):
            index = side * heads + head
            lanes = lane_block(index, DV)
            val = conv_rows(value[:, lanes].astype(F32), zero, conv_value[:, lanes].astype(F32))
            col = cols[:, head : head + 1]
            beta = cols[:, heads + head : heads + head + 1]
            beta_fade = cols[:, 2 * heads + head : 2 * heads + head + 1]
            lower = {}
            for i in range(parts):
                for j in range(i + 1):
                    a = slice(i * HALF, (i + 1) * HALF)
                    b = slice(j * HALF, (j + 1) * HALF)
                    spread = jnp.exp(jnp.minimum(col[a] - cumul[head : head + 1, b], 0.0))
                    entry = beta[a] * spread * dots[a, b]
                    lower[i, j] = jnp.where(below, entry, 0.0) if i == j else entry
            lowers.append(lower)
            rhs.append(jnp.concatenate([beta_fade * key, beta * val], 1))
            ends.append((key_t * to_end[head : head + 1]).astype(BF16))

    names = [(head, i) for head in range(heads) for i in range(parts)]
    tri = {}
    for head, i in names:
        near = (line // 2) == (across // 2)
        tri[head, i] = eye - jnp.where(near, lowers[head][i, i], 0.0)
    size = 2
    while size < HALF:
        mask = ((line // (2 * size)) == (across // (2 * size))) & ((line // size) != (across // size))
        low = {n: tri[n].astype(BF16) for n in names}
        inner = {
            (head, i): dot(jnp.where(mask, lowers[head][i, i], 0.0).astype(BF16), low[head, i]).astype(BF16)
            for head, i in names
        }
        tri = {n: tri[n] - dot(low[n], inner[n]) for n in names}
        size *= 2
    tri = {n: tri[n].astype(BF16) for n in names}
    solved = [[] for _ in range(heads)]
    for i in range(parts):
        for head in range(heads):
            need = rhs[head][i * HALF : (i + 1) * HALF]
            for j in range(i):
                need = need - fine_dot(lowers[head][i, j], solved[head][j])
            solved[head].append(dot(tri[head, i], need.astype(BF16)))
    for head in range(heads):
        both = jnp.concatenate(solved[head], 0).astype(BF16)
        solved_out[head] = both
        ended = dot(ends[head], both)
        fade_end = fade[head : head + 1, rows - 1 : rows]
        own = jnp.concatenate([eye * fade_end - ended[:, :KD], ended[:, KD:]], 1)
        maps_out[head] = own


def front_kernel(
    own, place, qk, value, halo, hist_qk, hist_value, conv_qk, conv_value, rest, cols,
    maps_out, keys_out, solved_out, hist_s, conv_s, hist_v,
):
    heads = rest.shape[0]
    key_heads = heads // 2
    key_cols = qk.shape[2]
    taps = conv_value.shape[0]
    count = taps - 1
    first = place[0] == 0
    side = place[1] if own else 1 - place[1]
    load_small(hist_qk, conv_qk, 1, hist_s, conv_s)
    hist_v[HALO - count :, :] = hist_value[...].astype(F32)
    for pair in range(key_heads):
        index = side * key_heads + pair
        lanes = lane_block(index, KD)
        key = unit_rows(
            front_rows(
                qk[1, :HALO, lanes], halo, hist_s, conv_s[:, lanes], lanes,
                lane_block(key_cols // KD + index, KD), first,
            )
        )
        keys = [key[i : i + 1] for i in range(count)]
        keys_out[pair] = stacked(keys, KD)
        dots = {
            (i, j): jnp.sum(keys[i] * keys[j], axis=-1, keepdims=True)
            for i in range(count)
            for j in range(i)
        }
        for head in (2 * pair, 2 * pair + 1):
            index = side * heads + head
            lanes = lane_block(index, DV)
            val = front_rows(
                value[:HALO, lanes], halo, hist_v, conv_value[:, lanes].astype(F32), lanes,
                lane_block(2 * key_cols // DV + index, DV), first,
            )
            beta = cols[:HALO, 4 * heads + head : 4 * heads + head + 1]
            cumul = running(cols[:HALO, 5 * heads + head : 5 * heads + head + 1], count)
            solved = []
            for i in range(count):
                need = jnp.concatenate([jnp.exp(cumul[i]) * keys[i], val[i : i + 1]], 1)
                for j in range(i):
                    need = need - (jnp.exp(cumul[i] - cumul[j]) * dots[i, j]) * solved[j]
                solved.append(beta[i : i + 1] * need)
            solved_out[head] = stacked(solved, KD + DV)
            ends = stacked([jnp.exp(cumul[-1] - cumul[i]) * keys[i] for i in range(count)], KD)
            maps_out[head] = put_ahead(rest[head], jnp.exp(cumul[-1]), ends, solved_out[head]).astype(BF16)


def put_ahead(rest, fade, ends, solved):
    through = dot_nt(rest[:, :KD].astype(BF16), ends.astype(BF16)).astype(BF16)
    moved = dot(through, solved.astype(BF16))
    return jnp.concatenate([fade * rest[:, :KD] - moved[:, :KD], rest[:, KD:] + moved[:, KD:]], 1)


def query_kernel(
    own, place, qk, halo, hist_qk, conv_qk, keys, solved, cumul, cols, front_keys, front_solved,
    gate_z, gain, reads_out, local_out, gate_out, hist_s, conv_s,
):
    heads, rows = cumul.shape
    key_heads = heads // 2
    count = conv_qk.shape[0] - 1
    first = place[0] == 0
    side = place[1] if own else 1 - place[1]
    load_small(hist_qk, conv_qk, 0, hist_s, conv_s)
    line = lax.broadcasted_iota(jnp.int32, (rows, rows), 0)
    across = lax.broadcasted_iota(jnp.int32, (rows, rows), 1)
    within = line >= across
    in_front = lax.broadcasted_iota(jnp.int32, (HALO, 1), 0) < count
    zero = jnp.zeros((HALO, KD), F32)
    for pair in range(key_heads):
        lanes = lane_block(side * key_heads + pair, KD)
        query = unit_rows(conv_rows(qk[0, :, lanes].astype(F32), zero, conv_s[:, lanes]))
        query = query * (KD**-0.5)
        ahead = unit_rows(
            front_rows(qk[0, :HALO, lanes], halo, hist_s, conv_s[:, lanes], lanes, lanes, first)
        ) * (KD**-0.5)
        dots = dot_nt(query.astype(BF16), keys[pair])
        front = [front_keys[pair, i : i + 1] for i in range(count)]
        for head in (2 * pair, 2 * pair + 1):
            col = cols[:, head : head + 1]
            fade = cols[:, 3 * heads + head : 3 * heads + head + 1]
            spread = jnp.exp(jnp.minimum(col - cumul[head : head + 1], 0.0))
            attend = jnp.where(within, spread * dots, 0.0).astype(BF16)
            part = dot(attend, solved[head])
            reads = jnp.concatenate([fade * query - part[:, :KD], part[:, KD:]], 1)
            sums = running(cols[:HALO, 5 * heads + head : 5 * heads + head + 1], count)
            ends = stacked([jnp.exp(sums[-1] - sums[i]) * front[i] for i in range(count)], KD)
            reads = put_ahead(reads, jnp.exp(sums[-1]), ends, front_solved[head])
            first_rows = []
            for i in range(count):
                asked = ahead[i : i + 1]
                row = jnp.concatenate([jnp.exp(sums[i]) * asked, jnp.zeros((1, DV), F32)], 1)
                for j in range(i + 1):
                    weight = jnp.exp(sums[i] - sums[j]) * jnp.sum(
                        asked * front[j], axis=-1, keepdims=True
                    )
                    term = weight * front_solved[head, j : j + 1]
                    row = row + jnp.concatenate([-term[:, :KD], term[:, KD:]], 1)
                first_rows.append(row)
            top = jnp.where(in_front, stacked(first_rows, KD + DV), reads[:HALO])
            reads = jnp.concatenate([top, reads[HALO:]], 0)
            reads_out[head] = reads[:, :KD].astype(BF16)
            local_out[head] = reads[:, KD:]
            lanes = lane_block(side * heads + head, DV)
            gate_out[head] = silu(gate_z[:, lanes].astype(F32)) * gain[...]


def join(outer, inner):
    product = dot(outer[:, :KD], inner)
    return jnp.concatenate([product[:, :KD], product[:, KD:] + outer[:, KD:].astype(F32)], 1)


def act(outer, state):
    return dot(outer[:, :KD], state) + outer[:, KD:].astype(F32)


def in_order(bit, mine, other, body):
    @pl.when(bit == 1)
    def _():
        body(other, mine)

    @pl.when(bit == 0)
    def _():
        body(mine, other)


def pair_kernel(place, maps, received, total_out):
    def body(low, high):
        for j in range(received.shape[0]):
            total_out[j] = join(high[j], low[j]).astype(BF16)

    in_order(place[1], maps, received, body)


def level_kernel(level, last, *refs):
    if level == 1:
        place, total, received, state_in, total_out, prefix_out = refs
        prefix = None
    else:
        place, total, received, prefix, state_in, total_out, prefix_out = refs
    half = total.shape[0]
    bit = place[level + 1]

    def body(low, high):
        for j in range(half):
            if last:
                state = state_in[place[1] * half + j].astype(BF16)
                total_out[j] = act(high[j], act(low[j], state).astype(BF16)).astype(BF16)
            else:
                total_out[j] = join(high[j], low[j]).astype(BF16)

    in_order(bit, total, received, body)

    @pl.when(bit == 1)
    def _():
        for j in range(half):
            if prefix is None:
                prefix_out[j] = received[j]
            else:
                prefix_out[j] = join(prefix[j], received[j]).astype(BF16)

    @pl.when(bit == 0)
    def _():
        line = lax.broadcasted_iota(jnp.int32, (KD, KD + DV), 0)
        across = lax.broadcasted_iota(jnp.int32, (KD, KD + DV), 1)
        same = jnp.where(line == across, 1.0, 0.0).astype(BF16)
        for j in range(half):
            prefix_out[j] = same if prefix is None else prefix[j]


def enter_kernel(top, place, prefix, state_in, came, maps, received, mine_out, send_out):
    bit = place[1]
    half = prefix.shape[0]

    @pl.when(place[top + 1] == 1)
    def _():
        for j in range(half):
            mine_out[j] = act(prefix[j], came[j]).astype(BF16)

    @pl.when(place[top + 1] == 0)
    def _():
        for j in range(half):
            mine_out[j] = act(prefix[j], state_in[bit * half + j].astype(BF16)).astype(BF16)

    @pl.when(bit == 1)
    def _():
        for j in range(half):
            entering = mine_out[j]
            send_out[j] = entering
            mine_out[j] = act(received[j], entering).astype(BF16)

    @pl.when(bit == 0)
    def _():
        for j in range(half):
            send_out[j] = act(maps[j], mine_out[j]).astype(BF16)


def normed_rows(local_part, reads, gate, state):
    out = local_part + dot(reads, state)
    scale = lax.rsqrt(jnp.mean(out * out, axis=-1, keepdims=True) + 1e-06)
    return (out * scale * gate).astype(BF16)


def project(side, rows_in, own, w_out, away, emit):
    core, bit, lift = side[0], side[1], side[2]
    depth = w_out.shape[0] // 2
    member = bit if own else 1 - bit
    width = w_out.shape[1] // emit.count
    for j in range(emit.count // 4):
        block = 2 * j + (1 - lift if away else lift)
        for target, column in ((0, 1 - core), (1, core)):
            lanes = lane_block(2 * block + column, width)
            rows_of = pl.ds(pl.multiple_of(member * depth, depth), depth)
            emit(target, j, dot(rows_in[...], w_out[rows_of, lanes]))


class Emit:
    def __init__(self, count, store):
        self.count, self.store = count, store

    def __call__(self, target, j, product):
        self.store(target, j, product)


def normed_all(states, reads, local_reads, gate, normed_out):
    for j in range(states.shape[0]):
        normed_out[:, j * DV : (j + 1) * DV] = normed_rows(
            local_reads[j], reads[j], gate[j], states[j]
        )


def own_kernel(side, states, reads, local_reads, gate, w_out, normed_out, far_out):
    normed_all(states, reads, local_reads, gate, normed_out)
    count = w_out.shape[1] // far_out.shape[3]

    def store(target, j, product):
        far_out[target, j] = product

    project(side, normed_out, True, w_out, True, Emit(count, store))


def away_kernel(
    side, states, reads, local_reads, gate, far, w_out, other_rows, send_out, keep_out
):
    normed_all(states, reads, local_reads, gate, other_rows)
    count = w_out.shape[1] // send_out.shape[2]

    def store(target, j, product):
        (send_out, keep_out)[target][j] = (far[target, j] + product).astype(BF16)

    project(side, other_rows, False, w_out, True, Emit(count, store))


def home_kernel(
    side, mine_rows, other_rows, w_out, maps, states, away_maps, away_states,
    send_out, keep_out, checkpoint,
):
    count = w_out.shape[1] // send_out.shape[2]
    sums = {}

    def store_own(target, j, product):
        sums[target, j] = product

    def store(target, j, product):
        (send_out, keep_out)[target][j] = (sums[target, j] + product).astype(BF16)

    project(side, mine_rows, True, w_out, False, Emit(count, store_own))
    project(side, other_rows, False, w_out, False, Emit(count, store))
    bit = side[1]
    half = maps.shape[0]
    for j in range(half):
        checkpoint[0, bit * half + j] = act(maps[j], states[j])
        checkpoint[0, (1 - bit) * half + j] = act(away_maps[j], away_states[j])


def swapped(value, axis, step):
    count = lax.axis_size(axis)
    return lax.ppermute(value, axis, [(i, i ^ step) for i in range(count)])


def local(
    hidden_in, w_qk, w_value, w_outgate, w_ba, conv_qk, conv_value, hist_qk, hist_value,
    a_log, dt_bias, beta_bias, state_in, norm_gain, w_out,
):
    rows, width = hidden_in.shape
    key_cols = w_qk.shape[2]
    heads = a_log.shape[0]
    half = heads // 2
    taps = conv_value.shape[0]
    n_seq = lax.axis_size("seq")
    n_head = lax.axis_size("head")
    levels = n_seq.bit_length() - 1
    seq = lax.axis_index("seq")
    col = lax.axis_index("head")

    def scalar(value):
        return value.astype(jnp.int32).reshape(1)

    place = {0: scalar(seq)} | {i + 1: scalar((seq >> i) & 1) for i in range(levels)}

    def only(*names):
        return {name: place[name] for name in names}


    qk = jnp.einsum("td,dce->cte", hidden_in, w_qk, preferred_element_type=F32).astype(BF16)
    value = jnp.dot(hidden_in, w_value, preferred_element_type=F32).astype(BF16)
    tail = rows - TAIL
    ends = jnp.concatenate([qk[0, tail:], qk[1, tail:], value[tail:]], 1)
    halo = lax.ppermute(ends, "seq", [(i, (i + 1) % n_seq) for i in range(n_seq)])
    gates = jnp.einsum("td,dch->cht", hidden_in, w_ba, preferred_element_type=F32).astype(BF16)

    small = [pltpu.VMEM((HALO, key_cols), F32), pltpu.VMEM((taps, key_cols), F32)]

    def prepare(own, qk):
        return call(
            functools.partial(prepare_kernel, own),
            (
                shape((half // 2, rows, KD), BF16),
                shape((half, rows, KD + DV), BF16),
                shape((half, KD, KD + DV), F32),
                shape((half, rows), F32),
                shape((rows, 128), F32),
            ),
            [VMEM] * 8,
            4 * 10**9,
            4 << 20,
            small[1:],
            only(1),
        )(
            a_log.reshape(1, heads), dt_bias.reshape(1, heads), beta_bias.reshape(1, heads),
            qk, value, gates, conv_qk, conv_value,
        )

    def front(own, prepared):
        return call(
            functools.partial(front_kernel, own),
            (
                shape((half, KD, KD + DV), BF16),
                shape((half // 2, HALO, KD), F32),
                shape((half, HALO, KD + DV), F32),
            ),
            [VMEM] * 9,
            10**8,
            1 << 20,
            small + [pltpu.VMEM((HALO, heads * DV), F32)],
            only(0, 1),
        )(
            qk, value, halo, hist_qk, hist_value, conv_qk, conv_value,
            prepared[2], prepared[4],
        )

    def query(own, prepared, fronted, qk):
        keys, solved, _, cumul, cols = prepared
        return call(
            functools.partial(query_kernel, own),
            (
                shape((half, rows, KD), BF16),
                shape((half, rows, DV), F32),
                shape((half, rows, DV), F32),
            ),
            [VMEM] * 12,
            2 * 10**9,
            4 << 20,
            small,
            only(0, 1),
        )(
            qk, halo, hist_qk, conv_qk, keys, solved, cumul, cols, fronted[1], fronted[2],
            gate_z, norm_gain.reshape(1, DV),
        )

    away = prepare(False, qk)
    halo, away = lax.optimization_barrier((halo, away))
    away_front = front(False, away)
    received = swapped(away_front[0], "seq", 1)
    later, _ = lax.optimization_barrier((qk, away_front[0]))
    own = prepare(True, later)
    own_front = front(True, own)
    maps, away_maps = own_front[0], away_front[0]
    received, own, maps = lax.optimization_barrier((received, own, maps))

    map_shape = shape((half, KD, KD + DV), BF16)
    state_shape = shape((half, KD, DV), BF16)
    total = call(
        pair_kernel, map_shape, [VMEM, VMEM], 10**8, 1 << 20, flags=only(1)
    )(maps, received)
    prefix = ()
    for level in range(1, levels - 1):
        other = swapped(total, "seq", 1 << level)
        if level == 1:
            later, _ = lax.optimization_barrier((hidden_in, total))
            gate_z = jnp.dot(later, w_outgate, preferred_element_type=F32).astype(BF16)
            other, gate_z = lax.optimization_barrier((other, gate_z))
        last = level == levels - 2
        total, prefix = call(
            functools.partial(level_kernel, level, last),
            (state_shape if last else map_shape, map_shape),
            [VMEM] * (3 if level == 1 else 4),
            10**8,
            1 << 20,
            flags=only(1, level + 1),
        )(total, other, *prefix, state_in)
        prefix = (prefix,)
    came = swapped(total, "seq", 1 << (levels - 1))
    later, _ = lax.optimization_barrier((qk, total))
    own_reads = query(True, own, own_front, later)
    away_reads = query(False, away, away_front, later)
    came, own_reads, away_reads = lax.optimization_barrier((came, own_reads, away_reads))
    mine, send_state = call(
        functools.partial(enter_kernel, levels - 1),
        (state_shape, state_shape),
        [VMEM] * 5,
        10**8,
        1 << 20,
        flags=only(1, levels),
    )(prefix[0], state_in, came, maps, received)
    other_state = swapped(send_state, "seq", 1)

    out_width = w_out.shape[1] // n_head
    blocks = n_head // 4
    side = {0: scalar(col & 1), 1: place[1], 2: scalar((col >> 1) & 1)}
    part_shape = shape((blocks, rows, out_width), BF16)
    rows_shape = shape((rows, half * DV), BF16)
    own_rows, far = call(
        own_kernel,
        (rows_shape, shape((2, blocks, rows, out_width), F32)),
        [VMEM] * 5,
        10**9,
        4 << 20,
        flags=side,
    )(mine, *own_reads, w_out)
    other_rows, send_out, keep = call(
        away_kernel,
        (rows_shape, part_shape, part_shape),
        [VMEM] * 6,
        10**9,
        4 << 20,
        flags=side,
    )(other_state, *away_reads, far, w_out)
    came_out = swapped(send_out, "head", 1)
    total_out = (keep.astype(F32) + came_out.astype(F32)).astype(BF16)
    total_out, other_rows = lax.optimization_barrier((total_out, other_rows))
    came_far = swapped(total_out, "head", 2)
    send_out, keep, checkpoint = call(
        home_kernel,
        (part_shape, part_shape, shape((1, heads, KD, DV), F32)),
        [VMEM] * 7,
        10**9,
        4 << 20,
        flags=side,
    )(own_rows, other_rows, w_out, maps, mine, away_maps, other_state)
    came_out = swapped(send_out, "head", 1)
    mixed = keep.astype(F32) + came_out.astype(F32) + came_far.astype(F32)
    step = 4
    while step < n_head:
        here = (col // step) & 1
        blocks //= 2
        pairs = mixed.reshape(blocks, 2, rows, out_width)
        send_out = lax.dynamic_index_in_dim(pairs, 1 - here, 1, False).astype(BF16)
        mixed = lax.dynamic_index_in_dim(pairs, here, 1, False)
        mixed = mixed + swapped(send_out, "head", step).astype(F32)
        step *= 2
    return (mixed[0].astype(BF16), checkpoint)


def solution(mesh):
    return jax.shard_map(
        local,
        mesh=mesh,
        in_specs=(
            P("seq", None),
            P(None, None, "head"),
            P(None, "head"),
            P(None, "head"),
            P(None, None, "head"),
            P(None, None, "head"),
            P(None, "head"),
            P(None, None, "head"),
            P(None, "head"),
            P("head"),
            P("head"),
            P("head"),
            P("head", None, None),
            P(),
            P("head", None),
        ),
        out_specs=(P("seq", "head"), P("seq", "head", None, None)),
        check_vma=False,
    )
```

```python
import functools

import jax
import jax.numpy as jnp
from jax import lax
from jax.experimental import pallas as pl
from jax.experimental.pallas import tpu as pltpu
from jax.sharding import PartitionSpec as P

KD = 128
DV = 128
HALF = 128
HALO = 16
TAIL = 8
F32 = jnp.float32
BF16 = jnp.bfloat16
VMEM = pl.BlockSpec(memory_space=pltpu.VMEM)
SMEM = pl.BlockSpec(memory_space=pltpu.SMEM)


def dot(left, right):
    return jnp.dot(left, right, preferred_element_type=F32)


def dot_nt(left, right):
    return lax.dot_general(left, right, (((1,), (1,)), ((), ())), preferred_element_type=F32)


def split(values):
    high = values.astype(BF16)
    return high, (values - high.astype(F32)).astype(BF16)


def fine_dot(left, right):
    left_hi, left_lo = split(left)
    right_hi, right_lo = split(right)
    return dot(left_hi, right_hi) + (dot(left_hi, right_lo) + dot(left_lo, right_hi))


def silu(values):
    return values / (1.0 + jnp.exp(-values))


def unit_rows(values):
    return values * lax.rsqrt(jnp.sum(values * values, axis=-1, keepdims=True) + 1e-06)


def conv_rows(block, halo, weight):
    rows = block.shape[0]
    taps = weight.shape[0]
    start = HALO - (taps - 1)
    joined = jnp.concatenate([halo, block], 0)
    total = weight[0:1] * joined[start : start + rows]
    for tap in range(1, taps):
        total = total + weight[tap : tap + 1] * joined[start + tap : start + tap + rows]
    return silu(total)


class Flags:
    def __init__(self, names, refs):
        self.refs = dict(zip(names, refs))

    def __getitem__(self, name):
        return self.refs[name][0]


def call(kernel, out_shape, in_specs, flops, moved, scratch=(), flags=None):
    names = tuple(flags or ())

    def body(*refs):
        if names:
            kernel(Flags(names, refs[: len(names)]), *refs[len(names) :])
        else:
            kernel(*refs)

    run = pl.pallas_call(
        body,
        out_shape=out_shape,
        in_specs=[SMEM] * len(names) + in_specs,
        out_specs=jax.tree.map(lambda _: VMEM, out_shape),
        scratch_shapes=list(scratch),
        compiler_params=pltpu.CompilerParams(vmem_limit_bytes=12 << 20),
        cost_estimate=pl.CostEstimate(flops=6 * flops, bytes_accessed=6 * moved, transcendentals=0),
    )
    return lambda *args: run(*[flags[name] for name in names], *args)


def shape(dims, dtype):
    return jax.ShapeDtypeStruct(dims, dtype)


def lane_block(index, width):
    return pl.ds(pl.multiple_of(index * width, width), width)


def picked(flag, values):
    count = values.shape[0] // 2
    return jnp.where(flag == 1, values[count:], values[:count])


def as_column(row):
    count = row.shape[1]
    line = lax.broadcasted_iota(jnp.int32, (count, count), 0)
    across = lax.broadcasted_iota(jnp.int32, (count, count), 1)
    return jnp.sum(jnp.where(line == across, row, 0.0), axis=1, keepdims=True)


def load_small(hist_qk, conv_qk, part, hist_s, conv_s):
    taps = conv_qk.shape[0]
    if hist_s is not None:
        hist_s[HALO - taps + 1 :, :] = hist_qk[...].astype(F32)[:, part, :]
    conv_s[...] = conv_qk[...].astype(F32)[:, part, :]


def front_rows(block, halo, hist, weight, lanes, halo_lanes, first):
    before = jnp.where(first, hist[HALO - TAIL :, lanes], halo[:, halo_lanes].astype(F32))
    pad = jnp.zeros((HALO - TAIL, before.shape[1]), F32)
    return conv_rows(block.astype(F32), jnp.concatenate([pad, before], 0), weight)


def running(column, count):
    sums = [column[0:1]]
    for i in range(1, count):
        sums.append(sums[-1] + column[i : i + 1])
    return sums


def stacked(rows_in, width):
    return jnp.concatenate(rows_in + [jnp.zeros((HALO - len(rows_in), width), F32)], 0)


def prepare_kernel(
    own, place, a_log, dt_bias, beta_bias, qk, value, gates, conv_qk, conv_value,
    keys_out, solved_out, maps_out, rows_out, cols_out, conv_s,
):
    heads = gates.shape[1] // 2
    rows = gates.shape[2]
    key_heads = heads // 2
    taps = conv_value.shape[0]
    side = place[1] if own else 1 - place[1]
    load_small(None, conv_qk, 1, None, conv_s)
    zero = jnp.zeros((HALO, KD), F32)
    rest = lax.broadcasted_iota(jnp.int32, (heads, rows), 1) >= taps - 1
    strength = jax.nn.sigmoid(
        picked(side, gates[0].astype(F32)) + picked(side, as_column(beta_bias[...]))
    )
    decay_in = picked(side, gates[1].astype(F32)) + picked(side, as_column(dt_bias[...]))
    soft = jnp.maximum(decay_in, 0.0) + jnp.log1p(jnp.exp(-jnp.abs(decay_in)))
    log_decay = -jnp.exp(picked(side, as_column(a_log[...]))) * soft
    raw = [strength, log_decay]
    strength = jnp.where(rest, strength, 0.0)
    log_decay = jnp.where(rest, log_decay, 0.0)
    line = lax.broadcasted_iota(jnp.int32, (rows, rows), 0)
    across = lax.broadcasted_iota(jnp.int32, (rows, rows), 1)
    upper = jnp.where(line <= across, 1.0, 0.0).astype(BF16)
    high, low = split(log_decay)
    lowest = (log_decay - high.astype(F32) - low.astype(F32)).astype(BF16)
    cumul = dot(high, upper) + (dot(low, upper) + dot(lowest, upper))
    fade = jnp.exp(cumul)
    to_end = jnp.exp(cumul[:, rows - 1 : rows] - cumul)
    pad = jnp.zeros((128 - 6 * heads, rows), F32)
    cols = jnp.concatenate([cumul, strength, strength * fade, fade, *raw, pad], 0).T
    rows_out[...] = cumul
    cols_out[...] = cols

    line = lax.broadcasted_iota(jnp.int32, (HALF, HALF), 0)
    across = lax.broadcasted_iota(jnp.int32, (HALF, HALF), 1)
    below = line > across
    eye = jnp.where(line == across, 1.0, 0.0)
    parts = rows // HALF
    lowers = []
    rhs = []
    ends = []
    for key_head in range(key_heads):
        lanes = lane_block(side * key_heads + key_head, KD)
        key = unit_rows(conv_rows(qk[1, :, lanes].astype(F32), zero, conv_s[:, lanes]))
        key_low = key.astype(BF16)
        keys_out[key_head] = key_low
        dots = dot_nt(key_low, key_low)
        key_t = key.T
        for head in (2 * key_head, 2 * key_head + 1):
            index = side * heads + head
            lanes = lane_block(index, DV)
            val = conv_rows(value[:, lanes].astype(F32), zero, conv_value[:, lanes].astype(F32))
            col = cols[:, head : head + 1]
            beta = cols[:, heads + head : heads + head + 1]
            beta_fade = cols[:, 2 * heads + head : 2 * heads + head + 1]
            lower = {}
            for i in range(parts):
                for j in range(i + 1):
                    a = slice(i * HALF, (i + 1) * HALF)
                    b = slice(j * HALF, (j + 1) * HALF)
                    spread = jnp.exp(jnp.minimum(col[a] - cumul[head : head + 1, b], 0.0))
                    entry = beta[a] * spread * dots[a, b]
                    lower[i, j] = jnp.where(below, entry, 0.0) if i == j else entry
            lowers.append(lower)
            rhs.append(jnp.concatenate([beta_fade * key, beta * val], 1))
            ends.append((key_t * to_end[head : head + 1]).astype(BF16))

    names = [(head, i) for head in range(heads) for i in range(parts)]
    tri = {}
    for head, i in names:
        near = (line // 2) == (across // 2)
        tri[head, i] = eye - jnp.where(near, lowers[head][i, i], 0.0)
    size = 2
    while size < HALF:
        mask = ((line // (2 * size)) == (across // (2 * size))) & ((line // size) != (across // size))
        low = {n: tri[n].astype(BF16) for n in names}
        inner = {
            (head, i): dot(jnp.where(mask, lowers[head][i, i], 0.0).astype(BF16), low[head, i]).astype(BF16)
            for head, i in names
        }
        tri = {n: tri[n] - dot(low[n], inner[n]) for n in names}
        size *= 2
    tri = {n: tri[n].astype(BF16) for n in names}
    solved = [[] for _ in range(heads)]
    for i in range(parts):
        for head in range(heads):
            need = rhs[head][i * HALF : (i + 1) * HALF]
            for j in range(i):
                need = need - fine_dot(lowers[head][i, j], solved[head][j])
            solved[head].append(dot(tri[head, i], need.astype(BF16)))
    for head in range(heads):
        both = jnp.concatenate(solved[head], 0).astype(BF16)
        solved_out[head] = both
        ended = dot(ends[head], both)
        fade_end = fade[head : head + 1, rows - 1 : rows]
        own = jnp.concatenate([eye * fade_end - ended[:, :KD], ended[:, KD:]], 1)
        maps_out[head] = own


def front_kernel(
    own, place, qk, value, halo, hist_qk, hist_value, conv_qk, conv_value, rest, cols,
    maps_out, keys_out, solved_out, hist_s, conv_s, hist_v,
):
    heads = rest.shape[0]
    key_heads = heads // 2
    key_cols = qk.shape[2]
    taps = conv_value.shape[0]
    count = taps - 1
    first = place[0] == 0
    side = place[1] if own else 1 - place[1]
    load_small(hist_qk, conv_qk, 1, hist_s, conv_s)
    hist_v[HALO - count :, :] = hist_value[...].astype(F32)
    for pair in range(key_heads):
        index = side * key_heads + pair
        lanes = lane_block(index, KD)
        key = unit_rows(
            front_rows(
                qk[1, :HALO, lanes], halo, hist_s, conv_s[:, lanes], lanes,
                lane_block(key_cols // KD + index, KD), first,
            )
        )
        keys = [key[i : i + 1] for i in range(count)]
        keys_out[pair] = stacked(keys, KD)
        dots = {
            (i, j): jnp.sum(keys[i] * keys[j], axis=-1, keepdims=True)
            for i in range(count)
            for j in range(i)
        }
        for head in (2 * pair, 2 * pair + 1):
            index = side * heads + head
            lanes = lane_block(index, DV)
            val = front_rows(
                value[:HALO, lanes], halo, hist_v, conv_value[:, lanes].astype(F32), lanes,
                lane_block(2 * key_cols // DV + index, DV), first,
            )
            beta = cols[:HALO, 4 * heads + head : 4 * heads + head + 1]
            cumul = running(cols[:HALO, 5 * heads + head : 5 * heads + head + 1], count)
            solved = []
            for i in range(count):
                need = jnp.concatenate([jnp.exp(cumul[i]) * keys[i], val[i : i + 1]], 1)
                for j in range(i):
                    need = need - (jnp.exp(cumul[i] - cumul[j]) * dots[i, j]) * solved[j]
                solved.append(beta[i : i + 1] * need)
            solved_out[head] = stacked(solved, KD + DV)
            ends = stacked([jnp.exp(cumul[-1] - cumul[i]) * keys[i] for i in range(count)], KD)
            maps_out[head] = put_ahead(rest[head], jnp.exp(cumul[-1]), ends, solved_out[head]).astype(BF16)


def put_ahead(rest, fade, ends, solved):
    through = dot_nt(rest[:, :KD].astype(BF16), ends.astype(BF16)).astype(BF16)
    moved = dot(through, solved.astype(BF16))
    return jnp.concatenate([fade * rest[:, :KD] - moved[:, :KD], rest[:, KD:] + moved[:, KD:]], 1)


def query_kernel(
    own, place, qk, halo, hist_qk, conv_qk, keys, solved, cumul, cols, front_keys, front_solved,
    gate_z, gain, reads_out, local_out, gate_out, hist_s, conv_s,
):
    heads, rows = cumul.shape
    key_heads = heads // 2
    count = conv_qk.shape[0] - 1
    first = place[0] == 0
    side = place[1] if own else 1 - place[1]
    load_small(hist_qk, conv_qk, 0, hist_s, conv_s)
    line = lax.broadcasted_iota(jnp.int32, (rows, rows), 0)
    across = lax.broadcasted_iota(jnp.int32, (rows, rows), 1)
    within = line >= across
    in_front = lax.broadcasted_iota(jnp.int32, (HALO, 1), 0) < count
    zero = jnp.zeros((HALO, KD), F32)
    for pair in range(key_heads):
        lanes = lane_block(side * key_heads + pair, KD)
        query = unit_rows(conv_rows(qk[0, :, lanes].astype(F32), zero, conv_s[:, lanes]))
        query = query * (KD**-0.5)
        ahead = unit_rows(
            front_rows(qk[0, :HALO, lanes], halo, hist_s, conv_s[:, lanes], lanes, lanes, first)
        ) * (KD**-0.5)
        dots = dot_nt(query.astype(BF16), keys[pair])
        front = [front_keys[pair, i : i + 1] for i in range(count)]
        for head in (2 * pair, 2 * pair + 1):
            col = cols[:, head : head + 1]
            fade = cols[:, 3 * heads + head : 3 * heads + head + 1]
            spread = jnp.exp(jnp.minimum(col - cumul[head : head + 1], 0.0))
            attend = jnp.where(within, spread * dots, 0.0).astype(BF16)
            part = dot(attend, solved[head])
            reads = jnp.concatenate([fade * query - part[:, :KD], part[:, KD:]], 1)
            sums = running(cols[:HALO, 5 * heads + head : 5 * heads + head + 1], count)
            ends = stacked([jnp.exp(sums[-1] - sums[i]) * front[i] for i in range(count)], KD)
            reads = put_ahead(reads, jnp.exp(sums[-1]), ends, front_solved[head])
            first_rows = []
            for i in range(count):
                asked = ahead[i : i + 1]
                row = jnp.concatenate([jnp.exp(sums[i]) * asked, jnp.zeros((1, DV), F32)], 1)
                for j in range(i + 1):
                    weight = jnp.exp(sums[i] - sums[j]) * jnp.sum(
                        asked * front[j], axis=-1, keepdims=True
                    )
                    term = weight * front_solved[head, j : j + 1]
                    row = row + jnp.concatenate([-term[:, :KD], term[:, KD:]], 1)
                first_rows.append(row)
            top = jnp.where(in_front, stacked(first_rows, KD + DV), reads[:HALO])
            reads = jnp.concatenate([top, reads[HALO:]], 0)
            reads_out[head] = reads[:, :KD].astype(BF16)
            local_out[head] = reads[:, KD:]
            lanes = lane_block(side * heads + head, DV)
            gate_out[head] = silu(gate_z[:, lanes].astype(F32)) * gain[...]


def join(outer, inner):
    product = dot(outer[:, :KD], inner)
    return jnp.concatenate([product[:, :KD], product[:, KD:] + outer[:, KD:].astype(F32)], 1)


def act(outer, state):
    return dot(outer[:, :KD], state) + outer[:, KD:].astype(F32)


def in_order(bit, mine, other, body):
    @pl.when(bit == 1)
    def _():
        body(other, mine)

    @pl.when(bit == 0)
    def _():
        body(mine, other)


def pair_kernel(place, maps, received, total_out):
    def body(low, high):
        for j in range(received.shape[0]):
            total_out[j] = join(high[j], low[j]).astype(BF16)

    in_order(place[1], maps, received, body)


def level_kernel(level, last, *refs):
    if level == 1:
        place, total, received, state_in, total_out, prefix_out = refs
        prefix = None
    else:
        place, total, received, prefix, state_in, total_out, prefix_out = refs
    half = total.shape[0]
    bit = place[level + 1]

    def body(low, high):
        for j in range(half):
            if last:
                state = state_in[place[1] * half + j].astype(BF16)
                total_out[j] = act(high[j], act(low[j], state).astype(BF16)).astype(BF16)
            else:
                total_out[j] = join(high[j], low[j]).astype(BF16)

    in_order(bit, total, received, body)

    @pl.when(bit == 1)
    def _():
        for j in range(half):
            if prefix is None:
                prefix_out[j] = received[j]
            else:
                prefix_out[j] = join(prefix[j], received[j]).astype(BF16)

    @pl.when(bit == 0)
    def _():
        line = lax.broadcasted_iota(jnp.int32, (KD, KD + DV), 0)
        across = lax.broadcasted_iota(jnp.int32, (KD, KD + DV), 1)
        same = jnp.where(line == across, 1.0, 0.0).astype(BF16)
        for j in range(half):
            prefix_out[j] = same if prefix is None else prefix[j]


def enter_kernel(top, place, prefix, state_in, came, maps, received, mine_out, send_out):
    bit = place[1]
    half = prefix.shape[0]

    @pl.when(place[top + 1] == 1)
    def _():
        for j in range(half):
            mine_out[j] = act(prefix[j], came[j]).astype(BF16)

    @pl.when(place[top + 1] == 0)
    def _():
        for j in range(half):
            mine_out[j] = act(prefix[j], state_in[bit * half + j].astype(BF16)).astype(BF16)

    @pl.when(bit == 1)
    def _():
        for j in range(half):
            entering = mine_out[j]
            send_out[j] = entering
            mine_out[j] = act(received[j], entering).astype(BF16)

    @pl.when(bit == 0)
    def _():
        for j in range(half):
            send_out[j] = act(maps[j], mine_out[j]).astype(BF16)


def normed_rows(local_part, reads, gate, state):
    out = local_part + dot(reads, state)
    scale = lax.rsqrt(jnp.mean(out * out, axis=-1, keepdims=True) + 1e-06)
    return (out * scale * gate).astype(BF16)


def project(side, rows_in, own, w_out, away, emit):
    core, bit, lift = side[0], side[1], side[2]
    depth = w_out.shape[0] // 2
    member = bit if own else 1 - bit
    width = w_out.shape[1] // emit.count
    for j in range(emit.count // 4):
        block = 2 * j + (1 - lift if away else lift)
        for target, column in ((0, 1 - core), (1, core)):
            lanes = lane_block(2 * block + column, width)
            rows_of = pl.ds(pl.multiple_of(member * depth, depth), depth)
            emit(target, j, dot(rows_in[...], w_out[rows_of, lanes]))


class Emit:
    def __init__(self, count, store):
        self.count, self.store = count, store

    def __call__(self, target, j, product):
        self.store(target, j, product)


def normed_all(states, reads, local_reads, gate, normed_out):
    for j in range(states.shape[0]):
        normed_out[:, j * DV : (j + 1) * DV] = normed_rows(
            local_reads[j], reads[j], gate[j], states[j]
        )


def own_kernel(side, states, reads, local_reads, gate, w_out, normed_out, far_out):
    normed_all(states, reads, local_reads, gate, normed_out)
    count = w_out.shape[1] // far_out.shape[3]

    def store(target, j, product):
        far_out[target, j] = product

    project(side, normed_out, True, w_out, True, Emit(count, store))


def away_kernel(
    side, states, reads, local_reads, gate, far, w_out, other_rows, send_out, keep_out
):
    normed_all(states, reads, local_reads, gate, other_rows)
    count = w_out.shape[1] // send_out.shape[2]

    def store(target, j, product):
        (send_out, keep_out)[target][j] = (far[target, j] + product).astype(BF16)

    project(side, other_rows, False, w_out, True, Emit(count, store))


def home_kernel(
    side, mine_rows, other_rows, w_out, maps, states, away_maps, away_states,
    send_out, keep_out, checkpoint,
):
    count = w_out.shape[1] // send_out.shape[2]
    sums = {}

    def store_own(target, j, product):
        sums[target, j] = product

    def store(target, j, product):
        (send_out, keep_out)[target][j] = (sums[target, j] + product).astype(BF16)

    project(side, mine_rows, True, w_out, False, Emit(count, store_own))
    project(side, other_rows, False, w_out, False, Emit(count, store))
    bit = side[1]
    half = maps.shape[0]
    for j in range(half):
        checkpoint[0, bit * half + j] = act(maps[j], states[j])
        checkpoint[0, (1 - bit) * half + j] = act(away_maps[j], away_states[j])


def swapped(value, axis, step):
    count = lax.axis_size(axis)
    return lax.ppermute(value, axis, [(i, i ^ step) for i in range(count)])


def local(
    hidden_in, w_qk, w_value, w_outgate, w_ba, conv_qk, conv_value, hist_qk, hist_value,
    a_log, dt_bias, beta_bias, state_in, norm_gain, w_out,
):
    rows, width = hidden_in.shape
    key_cols = w_qk.shape[2]
    heads = a_log.shape[0]
    half = heads // 2
    taps = conv_value.shape[0]
    n_seq = lax.axis_size("seq")
    n_head = lax.axis_size("head")
    levels = n_seq.bit_length() - 1
    seq = lax.axis_index("seq")
    col = lax.axis_index("head")

    def scalar(value):
        return value.astype(jnp.int32).reshape(1)

    place = {0: scalar(seq)} | {i + 1: scalar((seq >> i) & 1) for i in range(levels)}

    def only(*names):
        return {name: place[name] for name in names}


    qk = jnp.einsum("td,dce->cte", hidden_in, w_qk, preferred_element_type=F32).astype(BF16)
    value = jnp.dot(hidden_in, w_value, preferred_element_type=F32).astype(BF16)
    tail = rows - TAIL
    ends = jnp.concatenate([qk[0, tail:], qk[1, tail:], value[tail:]], 1)
    halo = lax.ppermute(ends, "seq", [(i, (i + 1) % n_seq) for i in range(n_seq)])
    gates = jnp.einsum("td,dch->cht", hidden_in, w_ba, preferred_element_type=F32).astype(BF16)

    small = [pltpu.VMEM((HALO, key_cols), F32), pltpu.VMEM((taps, key_cols), F32)]

    def prepare(own, qk):
        return call(
            functools.partial(prepare_kernel, own),
            (
                shape((half // 2, rows, KD), BF16),
                shape((half, rows, KD + DV), BF16),
                shape((half, KD, KD + DV), F32),
                shape((half, rows), F32),
                shape((rows, 128), F32),
            ),
            [VMEM] * 8,
            4 * 10**9,
            4 << 20,
            small[1:],
            only(1),
        )(
            a_log.reshape(1, heads), dt_bias.reshape(1, heads), beta_bias.reshape(1, heads),
            qk, value, gates, conv_qk, conv_value,
        )

    def front(own, prepared):
        return call(
            functools.partial(front_kernel, own),
            (
                shape((half, KD, KD + DV), BF16),
                shape((half // 2, HALO, KD), F32),
                shape((half, HALO, KD + DV), F32),
            ),
            [VMEM] * 9,
            10**8,
            1 << 20,
            small + [pltpu.VMEM((HALO, heads * DV), F32)],
            only(0, 1),
        )(
            qk, value, halo, hist_qk, hist_value, conv_qk, conv_value,
            prepared[2], prepared[4],
        )

    def query(own, prepared, fronted, qk):
        keys, solved, _, cumul, cols = prepared
        return call(
            functools.partial(query_kernel, own),
            (
                shape((half, rows, KD), BF16),
                shape((half, rows, DV), F32),
                shape((half, rows, DV), F32),
            ),
            [VMEM] * 12,
            2 * 10**9,
            4 << 20,
            small,
            only(0, 1),
        )(
            qk, halo, hist_qk, conv_qk, keys, solved, cumul, cols, fronted[1], fronted[2],
            gate_z, norm_gain.reshape(1, DV),
        )

    away = prepare(False, qk)
    halo, away = lax.optimization_barrier((halo, away))
    away_front = front(False, away)
    received = swapped(away_front[0], "seq", 1)
    later, _ = lax.optimization_barrier((qk, away_front[0]))
    own = prepare(True, later)
    own_front = front(True, own)
    maps, away_maps = own_front[0], away_front[0]
    received, own, maps = lax.optimization_barrier((received, own, maps))

    map_shape = shape((half, KD, KD + DV), BF16)
    state_shape = shape((half, KD, DV), BF16)
    total = call(
        pair_kernel, map_shape, [VMEM, VMEM], 10**8, 1 << 20, flags=only(1)
    )(maps, received)
    prefix = ()
    for level in range(1, levels - 1):
        other = swapped(total, "seq", 1 << level)
        if level == 1:
            later, _ = lax.optimization_barrier((hidden_in, total))
            gate_z = jnp.dot(later, w_outgate, preferred_element_type=F32).astype(BF16)
            other, gate_z = lax.optimization_barrier((other, gate_z))
        last = level == levels - 2
        total, prefix = call(
            functools.partial(level_kernel, level, last),
            (state_shape if last else map_shape, map_shape),
            [VMEM] * (3 if level == 1 else 4),
            10**8,
            1 << 20,
            flags=only(1, level + 1),
        )(total, other, *prefix, state_in)
        prefix = (prefix,)
    came = swapped(total, "seq", 1 << (levels - 1))
    later, _ = lax.optimization_barrier((qk, total))
    own_reads = query(True, own, own_front, later)
    away_reads = query(False, away, away_front, later)
    came, own_reads, away_reads = lax.optimization_barrier((came, own_reads, away_reads))
    mine, send_state = call(
        functools.partial(enter_kernel, levels - 1),
        (state_shape, state_shape),
        [VMEM] * 5,
        10**8,
        1 << 20,
        flags=only(1, levels),
    )(prefix[0], state_in, came, maps, received)
    other_state = swapped(send_state, "seq", 1)

    out_width = w_out.shape[1] // n_head
    blocks = n_head // 4
    side = {0: scalar(col & 1), 1: place[1], 2: scalar((col >> 1) & 1)}
    part_shape = shape((blocks, rows, out_width), BF16)
    rows_shape = shape((rows, half * DV), BF16)
    own_rows, far = call(
        own_kernel,
        (rows_shape, shape((2, blocks, rows, out_width), F32)),
        [VMEM] * 5,
        10**9,
        4 << 20,
        flags=side,
    )(mine, *own_reads, w_out)
    other_rows, send_out, keep = call(
        away_kernel,
        (rows_shape, part_shape, part_shape),
        [VMEM] * 6,
        10**9,
        4 << 20,
        flags=side,
    )(other_state, *away_reads, far, w_out)
    came_out = swapped(send_out, "head", 1)
    home_out, home_keep, checkpoint = call(
        home_kernel,
        (part_shape, part_shape, shape((1, heads, KD, DV), F32)),
        [VMEM] * 7,
        10**9,
        4 << 20,
        flags=side,
    )(own_rows, other_rows, w_out, maps, mine, away_maps, other_state)
    came_out, home_out = lax.optimization_barrier((came_out, home_out))
    total_out = (keep.astype(F32) + came_out.astype(F32)).astype(BF16)
    came_far = swapped(total_out, "head", 2)
    came_home = swapped(home_out, "head", 1)
    mixed = home_keep.astype(F32) + came_home.astype(F32) + came_far.astype(F32)
    step = 4
    while step < n_head:
        here = (col // step) & 1
        blocks //= 2
        pairs = mixed.reshape(blocks, 2, rows, out_width)
        send_out = lax.dynamic_index_in_dim(pairs, 1 - here, 1, False).astype(BF16)
        mixed = lax.dynamic_index_in_dim(pairs, here, 1, False)
        mixed = mixed + swapped(send_out, "head", step).astype(F32)
        step *= 2
    return (mixed[0].astype(BF16), checkpoint)


def solution(mesh):
    return jax.shard_map(
        local,
        mesh=mesh,
        in_specs=(
            P("seq", None),
            P(None, None, "head"),
            P(None, "head"),
            P(None, "head"),
            P(None, None, "head"),
            P(None, None, "head"),
            P(None, "head"),
            P(None, None, "head"),
            P(None, "head"),
            P("head"),
            P("head"),
            P("head"),
            P("head", None, None),
            P(),
            P("head", None),
        ),
        out_specs=(P("seq", "head"), P("seq", "head", None, None)),
        check_vma=False,
    )
```

```python
import functools

import jax
import jax.numpy as jnp
from jax import lax
from jax.experimental import pallas as pl
from jax.experimental.pallas import tpu as pltpu
from jax.sharding import PartitionSpec as P

KD = 128
DV = 128
HALF = 128
HALO = 16
TAIL = 8
ORDER = (3, 1, 2)
F32 = jnp.float32
BF16 = jnp.bfloat16
VMEM = pl.BlockSpec(memory_space=pltpu.VMEM)
SMEM = pl.BlockSpec(memory_space=pltpu.SMEM)


def dot(left, right):
    return jnp.dot(left, right, preferred_element_type=F32)


def dot_nt(left, right):
    return lax.dot_general(left, right, (((1,), (1,)), ((), ())), preferred_element_type=F32)


def split(values):
    high = values.astype(BF16)
    return high, (values - high.astype(F32)).astype(BF16)


def fine_dot(left, right):
    left_hi, left_lo = split(left)
    right_hi, right_lo = split(right)
    return dot(left_hi, right_hi) + (dot(left_hi, right_lo) + dot(left_lo, right_hi))


def silu(values):
    return values / (1.0 + jnp.exp(-values))


def unit_rows(values):
    return values * lax.rsqrt(jnp.sum(values * values, axis=-1, keepdims=True) + 1e-06)


def conv_rows(block, halo, weight):
    rows = block.shape[0]
    taps = weight.shape[0]
    start = HALO - (taps - 1)
    joined = jnp.concatenate([halo, block], 0)
    total = weight[0:1] * joined[start : start + rows]
    for tap in range(1, taps):
        total = total + weight[tap : tap + 1] * joined[start + tap : start + tap + rows]
    return silu(total)


class Flags:
    def __init__(self, names, refs):
        self.refs = dict(zip(names, refs))

    def __getitem__(self, name):
        return self.refs[name][0]


def call(kernel, out_shape, in_specs, flops, moved, scratch=(), flags=None):
    names = tuple(flags or ())

    def body(*refs):
        if names:
            kernel(Flags(names, refs[: len(names)]), *refs[len(names) :])
        else:
            kernel(*refs)

    run = pl.pallas_call(
        body,
        out_shape=out_shape,
        in_specs=[SMEM] * len(names) + in_specs,
        out_specs=jax.tree.map(lambda _: VMEM, out_shape),
        scratch_shapes=list(scratch),
        compiler_params=pltpu.CompilerParams(vmem_limit_bytes=12 << 20),
        cost_estimate=pl.CostEstimate(flops=flops, bytes_accessed=moved, transcendentals=0),
    )
    return lambda *args: run(*[flags[name] for name in names], *args)


def shape(dims, dtype):
    return jax.ShapeDtypeStruct(dims, dtype)


def lane_block(index, width):
    return pl.ds(pl.multiple_of(index * width, width), width)


def picked(flag, values):
    count = values.shape[0] // 2
    return jnp.where(flag == 1, values[count:], values[:count])


def as_column(row):
    count = row.shape[1]
    line = lax.broadcasted_iota(jnp.int32, (count, count), 0)
    across = lax.broadcasted_iota(jnp.int32, (count, count), 1)
    return jnp.sum(jnp.where(line == across, row, 0.0), axis=1, keepdims=True)


def load_small(hist_qk, conv_qk, part, hist_s, conv_s):
    taps = conv_qk.shape[0]
    if hist_s is not None:
        hist_s[HALO - taps + 1 :, :] = hist_qk[...].astype(F32)[:, part, :]
    conv_s[...] = conv_qk[...].astype(F32)[:, part, :]


def front_rows(block, halo, hist, weight, lanes, halo_lanes, first):
    before = jnp.where(first, hist[HALO - TAIL :, lanes], halo[:, halo_lanes].astype(F32))
    pad = jnp.zeros((HALO - TAIL, before.shape[1]), F32)
    return conv_rows(block.astype(F32), jnp.concatenate([pad, before], 0), weight)


def running(column, count):
    sums = [column[0:1]]
    for i in range(1, count):
        sums.append(sums[-1] + column[i : i + 1])
    return sums


def stacked(rows_in, width):
    return jnp.concatenate(rows_in + [jnp.zeros((HALO - len(rows_in), width), F32)], 0)


def prepare_kernel(
    a_log, dt_bias, beta_bias, qk, value, gates, conv_qk, conv_value,
    keys_out, solved_out, maps_out, rows_out, cols_out, conv_s,
):
    heads = gates.shape[1]
    rows = gates.shape[2]
    key_heads = heads // 2
    taps = conv_value.shape[0]
    load_small(None, conv_qk, 1, None, conv_s)
    zero = jnp.zeros((HALO, KD), F32)
    rest = lax.broadcasted_iota(jnp.int32, (heads, rows), 1) >= taps - 1
    strength = jax.nn.sigmoid(
        gates[0].astype(F32) + as_column(beta_bias[...])
    )
    decay_in = gates[1].astype(F32) + as_column(dt_bias[...])
    soft = jnp.maximum(decay_in, 0.0) + jnp.log1p(jnp.exp(-jnp.abs(decay_in)))
    log_decay = -jnp.exp(as_column(a_log[...])) * soft
    raw = [strength, log_decay]
    strength = jnp.where(rest, strength, 0.0)
    log_decay = jnp.where(rest, log_decay, 0.0)
    line = lax.broadcasted_iota(jnp.int32, (rows, rows), 0)
    across = lax.broadcasted_iota(jnp.int32, (rows, rows), 1)
    upper = jnp.where(line <= across, 1.0, 0.0).astype(BF16)
    high, low = split(log_decay)
    lowest = (log_decay - high.astype(F32) - low.astype(F32)).astype(BF16)
    cumul = dot(high, upper) + (dot(low, upper) + dot(lowest, upper))
    fade = jnp.exp(cumul)
    to_end = jnp.exp(cumul[:, rows - 1 : rows] - cumul)
    pad = jnp.zeros((128 - 6 * heads, rows), F32)
    cols = jnp.concatenate([cumul, strength, strength * fade, fade, *raw, pad], 0).T
    rows_out[...] = cumul
    cols_out[...] = cols

    line = lax.broadcasted_iota(jnp.int32, (HALF, HALF), 0)
    across = lax.broadcasted_iota(jnp.int32, (HALF, HALF), 1)
    below = line > across
    eye = jnp.where(line == across, 1.0, 0.0)
    parts = rows // HALF
    lowers = []
    rhs = []
    ends = []
    for key_head in range(key_heads):
        lanes = slice(key_head * KD, (key_head + 1) * KD)
        key = unit_rows(conv_rows(qk[1, :, lanes].astype(F32), zero, conv_s[:, lanes]))
        key_low = key.astype(BF16)
        keys_out[key_head] = key_low
        dots = dot_nt(key_low, key_low)
        key_t = key.T
        for head in (2 * key_head, 2 * key_head + 1):
            lanes = slice(head * DV, (head + 1) * DV)
            val = conv_rows(value[:, lanes].astype(F32), zero, conv_value[:, lanes].astype(F32))
            col = cols[:, head : head + 1]
            beta = cols[:, heads + head : heads + head + 1]
            beta_fade = cols[:, 2 * heads + head : 2 * heads + head + 1]
            lower = {}
            for i in range(parts):
                for j in range(i + 1):
                    a = slice(i * HALF, (i + 1) * HALF)
                    b = slice(j * HALF, (j + 1) * HALF)
                    spread = jnp.exp(jnp.minimum(col[a] - cumul[head : head + 1, b], 0.0))
                    entry = beta[a] * spread * dots[a, b]
                    lower[i, j] = jnp.where(below, entry, 0.0) if i == j else entry
            lowers.append(lower)
            rhs.append(jnp.concatenate([beta_fade * key, beta * val], 1))
            ends.append((key_t * to_end[head : head + 1]).astype(BF16))

    names = [(head, i) for head in range(heads) for i in range(parts)]
    tri = {}
    for head, i in names:
        near = (line // 2) == (across // 2)
        tri[head, i] = eye - jnp.where(near, lowers[head][i, i], 0.0)
    size = 2
    while size < HALF:
        mask = ((line // (2 * size)) == (across // (2 * size))) & ((line // size) != (across // size))
        low = {n: tri[n].astype(BF16) for n in names}
        inner = {
            (head, i): dot(jnp.where(mask, lowers[head][i, i], 0.0).astype(BF16), low[head, i]).astype(BF16)
            for head, i in names
        }
        tri = {n: tri[n] - dot(low[n], inner[n]) for n in names}
        size *= 2
    tri = {n: tri[n].astype(BF16) for n in names}
    solved = [[] for _ in range(heads)]
    for i in range(parts):
        for head in range(heads):
            need = rhs[head][i * HALF : (i + 1) * HALF]
            for j in range(i):
                need = need - fine_dot(lowers[head][i, j], solved[head][j])
            solved[head].append(dot(tri[head, i], need.astype(BF16)))
    for head in range(heads):
        both = jnp.concatenate(solved[head], 0).astype(BF16)
        solved_out[head] = both
        ended = dot(ends[head], both)
        fade_end = fade[head : head + 1, rows - 1 : rows]
        own = jnp.concatenate([eye * fade_end - ended[:, :KD], ended[:, KD:]], 1)
        maps_out[head] = own


def front_kernel(
    place, qk, value, halo, hist_qk, hist_value, conv_qk, conv_value, rest, cols,
    maps_out, keys_out, solved_out, send_1, send_2, send_3, hist_s, conv_s, hist_v,
):
    heads = rest.shape[0]
    key_heads = heads // 2
    key_cols = qk.shape[2]
    taps = conv_value.shape[0]
    count = taps - 1
    first = place["seq"] == 0
    load_small(hist_qk, conv_qk, 1, hist_s, conv_s)
    hist_v[HALO - count :, :] = hist_value[...].astype(F32)
    for pair in range(key_heads):
        lanes = slice(pair * KD, (pair + 1) * KD)
        halo_lanes = slice(key_cols + pair * KD, key_cols + (pair + 1) * KD)
        key = unit_rows(
            front_rows(
                qk[1, :HALO, lanes], halo, hist_s, conv_s[:, lanes], lanes, halo_lanes, first
            )
        )
        keys = [key[i : i + 1] for i in range(count)]
        keys_out[pair] = stacked(keys, KD)
        dots = {
            (i, j): jnp.sum(keys[i] * keys[j], axis=-1, keepdims=True)
            for i in range(count)
            for j in range(i)
        }
        for head in (2 * pair, 2 * pair + 1):
            lanes = slice(head * DV, (head + 1) * DV)
            halo_lanes = slice(2 * key_cols + head * DV, 2 * key_cols + (head + 1) * DV)
            val = front_rows(
                value[:HALO, lanes], halo, hist_v, conv_value[:, lanes].astype(F32), lanes,
                halo_lanes, first,
            )
            beta = cols[:HALO, 4 * heads + head : 4 * heads + head + 1]
            cumul = running(cols[:HALO, 5 * heads + head : 5 * heads + head + 1], count)
            solved = []
            for i in range(count):
                need = jnp.concatenate([jnp.exp(cumul[i]) * keys[i], val[i : i + 1]], 1)
                for j in range(i):
                    need = need - (jnp.exp(cumul[i] - cumul[j]) * dots[i, j]) * solved[j]
                solved.append(beta[i : i + 1] * need)
            solved_out[head] = stacked(solved, KD + DV)
            ends = stacked([jnp.exp(cumul[-1] - cumul[i]) * keys[i] for i in range(count)], KD)
            maps_out[head] = put_ahead(rest[head], jnp.exp(cumul[-1]), ends, solved_out[head]).astype(BF16)
    for other, send in ((1, send_1), (2, send_2), (3, send_3)):
        send[...] = maps_out[pl.ds((place["member"] ^ other) * (heads // 4), heads // 4)]


def put_ahead(rest, fade, ends, solved):
    through = dot_nt(rest[:, :KD].astype(BF16), ends.astype(BF16)).astype(BF16)
    moved = dot(through, solved.astype(BF16))
    return jnp.concatenate([fade * rest[:, :KD] - moved[:, :KD], rest[:, KD:] + moved[:, KD:]], 1)


def query_kernel(
    place, qk, halo, hist_qk, conv_qk, keys, solved, cumul, cols, front_keys, front_solved,
    reads_out, local_out, hist_s, conv_s,
):
    heads, rows = cumul.shape
    key_heads = heads // 2
    count = conv_qk.shape[0] - 1
    first = place["seq"] == 0
    load_small(hist_qk, conv_qk, 0, hist_s, conv_s)
    line = lax.broadcasted_iota(jnp.int32, (rows, rows), 0)
    across = lax.broadcasted_iota(jnp.int32, (rows, rows), 1)
    within = line >= across
    in_front = lax.broadcasted_iota(jnp.int32, (HALO, 1), 0) < count
    zero = jnp.zeros((HALO, KD), F32)
    for pair in range(key_heads):
        lanes = slice(pair * KD, (pair + 1) * KD)
        query = unit_rows(conv_rows(qk[0, :, lanes].astype(F32), zero, conv_s[:, lanes]))
        query = query * (KD**-0.5)
        ahead = unit_rows(
            front_rows(qk[0, :HALO, lanes], halo, hist_s, conv_s[:, lanes], lanes, lanes, first)
        ) * (KD**-0.5)
        dots = dot_nt(query.astype(BF16), keys[pair])
        front = [front_keys[pair, i : i + 1] for i in range(count)]
        for head in (2 * pair, 2 * pair + 1):
            col = cols[:, head : head + 1]
            fade = cols[:, 3 * heads + head : 3 * heads + head + 1]
            spread = jnp.exp(jnp.minimum(col - cumul[head : head + 1], 0.0))
            attend = jnp.where(within, spread * dots, 0.0).astype(BF16)
            part = dot(attend, solved[head])
            reads = jnp.concatenate([fade * query - part[:, :KD], part[:, KD:]], 1)
            sums = running(cols[:HALO, 5 * heads + head : 5 * heads + head + 1], count)
            ends = stacked([jnp.exp(sums[-1] - sums[i]) * front[i] for i in range(count)], KD)
            reads = put_ahead(reads, jnp.exp(sums[-1]), ends, front_solved[head])
            first_rows = []
            for i in range(count):
                asked = ahead[i : i + 1]
                row = jnp.concatenate([jnp.exp(sums[i]) * asked, jnp.zeros((1, DV), F32)], 1)
                for j in range(i + 1):
                    weight = jnp.exp(sums[i] - sums[j]) * jnp.sum(
                        asked * front[j], axis=-1, keepdims=True
                    )
                    term = weight * front_solved[head, j : j + 1]
                    row = row + jnp.concatenate([-term[:, :KD], term[:, KD:]], 1)
                first_rows.append(row)
            top = jnp.where(in_front, stacked(first_rows, KD + DV), reads[:HALO])
            reads = jnp.concatenate([top, reads[HALO:]], 0)
            reads_out[head] = reads[:, :KD].astype(BF16)
            local_out[head] = reads[:, KD:]


def join(outer, inner):
    product = dot(outer[:, :KD], inner)
    return jnp.concatenate([product[:, :KD], product[:, KD:] + outer[:, KD:].astype(F32)], 1)


def act(outer, state):
    return dot(outer[:, :KD], state) + outer[:, KD:].astype(F32)


def in_order(bit, mine, other, body):
    @pl.when(bit == 1)
    def _():
        body(other, mine)

    @pl.when(bit == 0)
    def _():
        body(mine, other)


def each_member(member, body):
    for i in range(4):
        pl.when(member == i)(functools.partial(body, i))


def group_kernel(last, place, maps, got_1, got_2, got_3, state_in, total_out):
    size = got_1.shape[0]

    def body(member):
        mine = [maps[member * size + j] for j in range(size)]
        every = (mine, got_1, got_2, got_3)
        for j in range(size):
            if last:
                total_out[j] = state_in[member * size + j].astype(BF16)
            else:
                total_out[j] = every[member][j]
        for step in range(0 if last else 1, 4):
            for j in range(size):
                apply = act if last else join
                total_out[j] = apply(every[step ^ member][j], total_out[j]).astype(BF16)

    each_member(place["member"], body)


def level_kernel(level, last, *refs):
    if level == 2:
        place, total, received, state_in, total_out, prefix_out = refs
        prefix = None
    else:
        place, total, received, prefix, state_in, total_out, prefix_out = refs
    size = total.shape[0]
    bit = place[level]

    def body(low, high):
        for j in range(size):
            if last:
                state = state_in[place["member"] * size + j].astype(BF16)
                total_out[j] = act(high[j], act(low[j], state).astype(BF16)).astype(BF16)
            else:
                total_out[j] = join(high[j], low[j]).astype(BF16)

    in_order(bit, total, received, body)

    @pl.when(bit == 1)
    def _():
        for j in range(size):
            if prefix is None:
                prefix_out[j] = received[j]
            else:
                prefix_out[j] = join(prefix[j], received[j]).astype(BF16)

    @pl.when(bit == 0)
    def _():
        line = lax.broadcasted_iota(jnp.int32, (KD, KD + DV), 0)
        across = lax.broadcasted_iota(jnp.int32, (KD, KD + DV), 1)
        same = jnp.where(line == across, 1.0, 0.0).astype(BF16)
        for j in range(size):
            prefix_out[j] = same if prefix is None else prefix[j]


def enter_kernel(place, maps, got_1, got_2, got_3, state_in, came, *refs):
    *prefix, mine_out, send_1, send_2, send_3 = refs
    size = came.shape[0]
    outs = (mine_out, send_1, send_2, send_3)

    @pl.when(place["top"] == 1)
    def _():
        mine_out[...] = came[...]

    @pl.when(place["top"] == 0)
    def _():
        for j in range(size):
            mine_out[j] = state_in[place["member"] * size + j].astype(BF16)

    if prefix:
        for j in range(size):
            mine_out[j] = act(prefix[0][j], mine_out[j]).astype(BF16)

    def body(member):
        mine = [maps[member * size + j] for j in range(size)]
        every = (mine, got_1, got_2, got_3)
        states = [mine_out[j] for j in range(size)]
        for step in range(4):
            for j in range(size):
                outs[step ^ member][j] = states[j]
            if step < 3:
                states = [
                    act(every[step ^ member][j], states[j]).astype(BF16) for j in range(size)
                ]

    each_member(place["member"], body)


def normed_rows(local_part, reads, gate, gain, state):
    out = local_part + dot(reads, state)
    scale = lax.rsqrt(jnp.mean(out * out, axis=-1, keepdims=True) + 1e-06)
    return (out * scale * gain * silu(gate.astype(F32))).astype(BF16)


def normed_slots(slots, place, states, reads, local_reads, gate_z, gain, normed_out):
    size = states[0].shape[0]
    for at, slot in enumerate(slots):
        for j in range(size):
            head = (place["member"] ^ slot) * size + j
            normed_out[at, :, j * DV : (j + 1) * DV] = normed_rows(
                local_reads[head], reads[head], gate_z[:, lane_block(head, DV)], gain[...],
                states[at][j],
            )


def project(slots, place, normed, w_out, lift, width, j, target):
    depth = normed.shape[2]
    column = place["core"] if target else 1 - place["core"]
    lanes = lane_block(2 * (2 * j + lift) + column, width)
    total = None
    for at, slot in enumerate(slots):
        rows_of = lane_block(place["member"] ^ slot, depth)
        product = dot(normed[at], w_out[rows_of, lanes])
        total = product if total is None else total + product
    return total


def early_kernel(slots, place, *refs):
    *states, reads, local_reads, gate_z, gain, normed_out = refs
    normed_slots(slots, place, states, reads, local_reads, gate_z, gain, normed_out)


def both_products(early, late, place, early_rows, late_rows, w_out, lift, width, j, target):
    return project(early, place, early_rows, w_out, lift, width, j, target) + project(
        late, place, late_rows, w_out, lift, width, j, target
    )


def late_kernel(early, late, place, *refs):
    *states, reads, local_reads, gate_z, gain, early_rows, w_out = refs[:-3]
    late_rows, send_out, keep_out = refs[-3:]
    normed_slots(late, place, states, reads, local_reads, gate_z, gain, late_rows)
    for target, out in enumerate((send_out, keep_out)):
        for j in range(out.shape[0]):
            out[j] = both_products(
                early, late, place, early_rows, late_rows, w_out, 1 - place["lift"], out.shape[2],
                j, target,
            ).astype(BF16)


def home_kernel(
    early, late, place, early_rows, late_rows, w_out, maps, state_0, state_1, state_2, state_3,
    send_out, keep_out, checkpoint,
):
    for target, out in enumerate((send_out, keep_out)):
        for j in range(out.shape[0]):
            total = both_products(
                early, late, place, early_rows, late_rows, w_out, place["lift"], out.shape[2],
                j, target,
            )
            out[j] = total.astype(BF16)
    size = state_0.shape[0]
    for slot, states in enumerate((state_0, state_1, state_2, state_3)):
        for j in range(size):
            head = (place["member"] ^ slot) * size + j
            checkpoint[0, head] = act(maps[head], states[j])


def swapped(value, axis, step):
    count = lax.axis_size(axis)
    return lax.ppermute(value, axis, [(i, i ^ step) for i in range(count)])


def local(
    hidden_in, w_qk, w_value, w_outgate, w_ba, conv_qk, conv_value, hist_qk, hist_value,
    a_log, dt_bias, beta_bias, state_in, norm_gain, w_out,
):
    rows, width = hidden_in.shape
    key_cols = w_qk.shape[2]
    heads = a_log.shape[0]
    half = heads // 2
    taps = conv_value.shape[0]
    n_seq = lax.axis_size("seq")
    n_head = lax.axis_size("head")
    levels = n_seq.bit_length() - 1
    seq = lax.axis_index("seq")
    col = lax.axis_index("head")

    def scalar(value):
        return value.astype(jnp.int32).reshape(1)

    place = {i: scalar((seq >> i) & 1) for i in range(levels)} | {
        "seq": scalar(seq),
        "member": scalar(seq & 3),
        "top": scalar(seq >> (levels - 1)),
        "core": scalar(col & 1),
        "lift": scalar((col >> 1) & 1),
    }

    def only(*names):
        return {name: place[name] for name in names}


    qk = jnp.einsum("td,dce->cte", hidden_in, w_qk, preferred_element_type=F32).astype(BF16)
    value = jnp.dot(hidden_in, w_value, preferred_element_type=F32).astype(BF16)
    tail = rows - TAIL
    ends = jnp.concatenate([qk[0, tail:], qk[1, tail:], value[tail:]], 1)
    halo = lax.ppermute(ends, "seq", [(i, (i + 1) % n_seq) for i in range(n_seq)])
    gates = jnp.einsum("td,dch->cht", hidden_in, w_ba, preferred_element_type=F32).astype(BF16)

    small = [pltpu.VMEM((HALO, key_cols), F32), pltpu.VMEM((taps, key_cols), F32)]

    size = heads // 4
    keys, solved, rest, cumul, cols = call(
        prepare_kernel,
        (
            shape((half, rows, KD), BF16),
            shape((heads, rows, KD + DV), BF16),
            shape((heads, KD, KD + DV), F32),
            shape((heads, rows), F32),
            shape((rows, 128), F32),
        ),
        [VMEM] * 8,
        10000000,
        25165824,
        small[1:],
    )(
        a_log.reshape(1, heads), dt_bias.reshape(1, heads), beta_bias.reshape(1, heads),
        qk, value, gates, conv_qk, conv_value,
    )
    halo, rest = lax.optimization_barrier((halo, rest))
    map_shape = shape((size, KD, KD + DV), BF16)
    state_shape = shape((size, KD, DV), BF16)
    maps, front_keys, front_solved, *sends = call(
        front_kernel,
        (
            shape((heads, KD, KD + DV), BF16),
            shape((half, HALO, KD), F32),
            shape((heads, HALO, KD + DV), F32),
            map_shape,
            map_shape,
            map_shape,
        ),
        [VMEM] * 9,
        10000000,
        50331648,
        small + [pltpu.VMEM((HALO, heads * DV), F32)],
        only("seq", "member"),
    )(qk, value, halo, hist_qk, hist_value, conv_qk, conv_value, rest, cols)

    def to_all(values):
        got = {step: swapped(values[step - 1], "seq", step) for step in ORDER}
        return [got[step] for step in (1, 2, 3)]

    got = to_all(sends)
    later, _ = lax.optimization_barrier((qk, maps))
    reads = call(
        query_kernel,
        (shape((heads, rows, KD), BF16), shape((heads, rows, DV), F32)),
        [VMEM] * 10,
        100000000000,
        6291456,
        small,
        only("seq"),
    )(later, halo, hist_qk, conv_qk, keys, solved, cumul, cols, front_keys, front_solved)
    got, reads = lax.optimization_barrier((got, reads))

    last = levels == 3
    total = call(
        functools.partial(group_kernel, last),
        state_shape if last else map_shape,
        [VMEM] * 5,
        24000000000,
        50331648,
        flags=only("member"),
    )(maps, *got, state_in)
    prefix = ()
    for level in range(2, levels - 1):
        other = swapped(total, "seq", 1 << level)
        last = level == levels - 2
        total, prefix = call(
            functools.partial(level_kernel, level, last),
            (state_shape if last else map_shape, map_shape),
            [VMEM] * (3 if level == 2 else 4),
            10**8,
            1 << 20,
            flags=only("member", level),
        )(total, other, *prefix, state_in)
        prefix = (prefix,)
    came = swapped(total, "seq", 1 << (levels - 1))
    later, _ = lax.optimization_barrier((hidden_in, total))
    gate_z = jnp.dot(later, w_outgate, preferred_element_type=F32).astype(BF16)
    came, gate_z = lax.optimization_barrier((came, gate_z))
    mine, *sends = call(
        enter_kernel,
        (state_shape,) * 4,
        [VMEM] * (6 + len(prefix)),
        600000000,
        25165824,
        flags=only("member", "top"),
    )(maps, *got, state_in, came, *prefix)
    states = [mine] + to_all(sends)

    out_width = w_out.shape[1] // n_head
    blocks = n_head // 4
    side = only("member", "core", "lift")
    part_shape = shape((blocks, rows, out_width), BF16)
    early, late = (0,) + ORDER[:2], ORDER[2:]
    gain = norm_gain.reshape(1, DV)
    early_rows = call(
        functools.partial(early_kernel, early),
        shape((len(early), rows, size * DV), BF16),
        [VMEM] * (4 + len(early)),
        1000000,
        25165824,
        flags=side,
    )(*[states[slot] for slot in early], *reads, gate_z, gain)
    late_rows, send_out, keep = call(
        functools.partial(late_kernel, early, late),
        (shape((len(late), rows, size * DV), BF16), part_shape, part_shape),
        [VMEM] * (6 + len(late)),
        100000000000,
        50331648,
        flags=side,
    )(*[states[slot] for slot in late], *reads, gate_z, gain, early_rows, w_out)
    came_out = swapped(send_out, "head", 1)
    home_out, home_keep, checkpoint = call(
        functools.partial(home_kernel, early, late),
        (part_shape, part_shape, shape((1, heads, KD, DV), F32)),
        [VMEM] * 8,
        6000000000,
        25165824,
        flags=side,
    )(early_rows, late_rows, w_out, maps, *states)
    came_out, home_out = lax.optimization_barrier((came_out, home_out))
    total_out = (keep.astype(F32) + came_out.astype(F32)).astype(BF16)
    came_far = swapped(total_out, "head", 2)
    came_home = swapped(home_out, "head", 1)
    mixed = home_keep.astype(F32) + came_home.astype(F32) + came_far.astype(F32)
    step = 4
    while step < n_head:
        here = (col // step) & 1
        blocks //= 2
        pairs = mixed.reshape(blocks, 2, rows, out_width)
        send_out = lax.dynamic_index_in_dim(pairs, 1 - here, 1, False).astype(BF16)
        mixed = lax.dynamic_index_in_dim(pairs, here, 1, False)
        mixed = mixed + swapped(send_out, "head", step).astype(F32)
        step *= 2
    return (mixed[0].astype(BF16), checkpoint)


def solution(mesh):
    return jax.shard_map(
        local,
        mesh=mesh,
        in_specs=(
            P("seq", None),
            P(None, None, "head"),
            P(None, "head"),
            P(None, "head"),
            P(None, None, "head"),
            P(None, None, "head"),
            P(None, "head"),
            P(None, None, "head"),
            P(None, "head"),
            P("head"),
            P("head"),
            P("head"),
            P("head", None, None),
            P(),
            P("head", None),
        ),
        out_specs=(P("seq", "head"), P("seq", "head", None, None)),
        check_vma=False,
    )
```

```python
import functools

import jax
import jax.numpy as jnp
from jax import lax
from jax.experimental import pallas as pl
from jax.experimental.pallas import tpu as pltpu
from jax.sharding import PartitionSpec as P

KD = 128
DV = 128
HALF = 128
HALO = 16
TAIL = 8
ORDER = (3, 1, 2)
F32 = jnp.float32
BF16 = jnp.bfloat16
VMEM = pl.BlockSpec(memory_space=pltpu.VMEM)
SMEM = pl.BlockSpec(memory_space=pltpu.SMEM)


def dot(left, right):
    return jnp.dot(left, right, preferred_element_type=F32)


def dot_nt(left, right):
    return lax.dot_general(left, right, (((1,), (1,)), ((), ())), preferred_element_type=F32)


def split(values):
    high = values.astype(BF16)
    return high, (values - high.astype(F32)).astype(BF16)


def fine_dot(left, right):
    left_hi, left_lo = split(left)
    right_hi, right_lo = split(right)
    return dot(left_hi, right_hi) + (dot(left_hi, right_lo) + dot(left_lo, right_hi))


def silu(values):
    return values / (1.0 + jnp.exp(-values))


def unit_rows(values):
    return values * lax.rsqrt(jnp.sum(values * values, axis=-1, keepdims=True) + 1e-06)


def conv_rows(block, halo, weight):
    rows = block.shape[0]
    taps = weight.shape[0]
    start = HALO - (taps - 1)
    joined = jnp.concatenate([halo, block], 0)
    total = weight[0:1] * joined[start : start + rows]
    for tap in range(1, taps):
        total = total + weight[tap : tap + 1] * joined[start + tap : start + tap + rows]
    return silu(total)


class Flags:
    def __init__(self, names, refs):
        self.refs = dict(zip(names, refs))

    def __getitem__(self, name):
        return self.refs[name][0]


def call(kernel, out_shape, in_specs, flops, moved, scratch=(), flags=None):
    names = tuple(flags or ())

    def body(*refs):
        if names:
            kernel(Flags(names, refs[: len(names)]), *refs[len(names) :])
        else:
            kernel(*refs)

    run = pl.pallas_call(
        body,
        out_shape=out_shape,
        in_specs=[SMEM] * len(names) + in_specs,
        out_specs=jax.tree.map(lambda _: VMEM, out_shape),
        scratch_shapes=list(scratch),
        compiler_params=pltpu.CompilerParams(vmem_limit_bytes=12 << 20),
        cost_estimate=pl.CostEstimate(flops=flops, bytes_accessed=moved, transcendentals=0),
    )
    return lambda *args: run(*[flags[name] for name in names], *args)


def shape(dims, dtype):
    return jax.ShapeDtypeStruct(dims, dtype)


def lane_block(index, width):
    return pl.ds(pl.multiple_of(index * width, width), width)


def picked(flag, values):
    count = values.shape[0] // 2
    return jnp.where(flag == 1, values[count:], values[:count])


def as_column(row):
    count = row.shape[1]
    line = lax.broadcasted_iota(jnp.int32, (count, count), 0)
    across = lax.broadcasted_iota(jnp.int32, (count, count), 1)
    return jnp.sum(jnp.where(line == across, row, 0.0), axis=1, keepdims=True)


def load_small(hist_qk, conv_qk, part, hist_s, conv_s):
    taps = conv_qk.shape[0]
    if hist_s is not None:
        hist_s[HALO - taps + 1 :, :] = hist_qk[...].astype(F32)[:, part, :]
    conv_s[...] = conv_qk[...].astype(F32)[:, part, :]


def front_rows(block, halo, hist, weight, lanes, halo_lanes, first):
    before = jnp.where(first, hist[HALO - TAIL :, lanes], halo[:, halo_lanes].astype(F32))
    pad = jnp.zeros((HALO - TAIL, before.shape[1]), F32)
    return conv_rows(block.astype(F32), jnp.concatenate([pad, before], 0), weight)


def running(column, count):
    sums = [column[0:1]]
    for i in range(1, count):
        sums.append(sums[-1] + column[i : i + 1])
    return sums


def stacked(rows_in, width):
    return jnp.concatenate(rows_in + [jnp.zeros((HALO - len(rows_in), width), F32)], 0)


def prepare_kernel(
    a_log, dt_bias, beta_bias, qk, value, gates, conv_qk, conv_value,
    keys_out, solved_out, maps_out, rows_out, cols_out, conv_s,
):
    heads = gates.shape[1]
    rows = gates.shape[2]
    key_heads = heads // 2
    taps = conv_value.shape[0]
    load_small(None, conv_qk, 1, None, conv_s)
    zero = jnp.zeros((HALO, KD), F32)
    rest = lax.broadcasted_iota(jnp.int32, (heads, rows), 1) >= taps - 1
    strength = jax.nn.sigmoid(
        gates[0].astype(F32) + as_column(beta_bias[...])
    )
    decay_in = gates[1].astype(F32) + as_column(dt_bias[...])
    soft = jnp.maximum(decay_in, 0.0) + jnp.log1p(jnp.exp(-jnp.abs(decay_in)))
    log_decay = -jnp.exp(as_column(a_log[...])) * soft
    raw = [strength, log_decay]
    strength = jnp.where(rest, strength, 0.0)
    log_decay = jnp.where(rest, log_decay, 0.0)
    line = lax.broadcasted_iota(jnp.int32, (rows, rows), 0)
    across = lax.broadcasted_iota(jnp.int32, (rows, rows), 1)
    upper = jnp.where(line <= across, 1.0, 0.0).astype(BF16)
    high, low = split(log_decay)
    lowest = (log_decay - high.astype(F32) - low.astype(F32)).astype(BF16)
    cumul = dot(high, upper) + (dot(low, upper) + dot(lowest, upper))
    fade = jnp.exp(cumul)
    to_end = jnp.exp(cumul[:, rows - 1 : rows] - cumul)
    pad = jnp.zeros((128 - 6 * heads, rows), F32)
    cols = jnp.concatenate([cumul, strength, strength * fade, fade, *raw, pad], 0).T
    rows_out[...] = cumul
    cols_out[...] = cols

    line = lax.broadcasted_iota(jnp.int32, (HALF, HALF), 0)
    across = lax.broadcasted_iota(jnp.int32, (HALF, HALF), 1)
    below = line > across
    eye = jnp.where(line == across, 1.0, 0.0)
    parts = rows // HALF
    lowers = []
    rhs = []
    ends = []
    for key_head in range(key_heads):
        lanes = slice(key_head * KD, (key_head + 1) * KD)
        key = unit_rows(conv_rows(qk[1, :, lanes].astype(F32), zero, conv_s[:, lanes]))
        key_low = key.astype(BF16)
        keys_out[key_head] = key_low
        dots = dot_nt(key_low, key_low)
        key_t = key.T
        for head in (2 * key_head, 2 * key_head + 1):
            lanes = slice(head * DV, (head + 1) * DV)
            val = conv_rows(value[:, lanes].astype(F32), zero, conv_value[:, lanes].astype(F32))
            col = cols[:, head : head + 1]
            beta = cols[:, heads + head : heads + head + 1]
            beta_fade = cols[:, 2 * heads + head : 2 * heads + head + 1]
            lower = {}
            for i in range(parts):
                for j in range(i + 1):
                    a = slice(i * HALF, (i + 1) * HALF)
                    b = slice(j * HALF, (j + 1) * HALF)
                    spread = jnp.exp(jnp.minimum(col[a] - cumul[head : head + 1, b], 0.0))
                    entry = beta[a] * spread * dots[a, b]
                    lower[i, j] = jnp.where(below, entry, 0.0) if i == j else entry
            lowers.append(lower)
            rhs.append(jnp.concatenate([beta_fade * key, beta * val], 1))
            ends.append((key_t * to_end[head : head + 1]).astype(BF16))

    names = [(head, i) for head in range(heads) for i in range(parts)]
    tri = {}
    for head, i in names:
        near = (line // 2) == (across // 2)
        tri[head, i] = eye - jnp.where(near, lowers[head][i, i], 0.0)
    size = 2
    while size < HALF:
        mask = ((line // (2 * size)) == (across // (2 * size))) & ((line // size) != (across // size))
        low = {n: tri[n].astype(BF16) for n in names}
        inner = {
            (head, i): dot(jnp.where(mask, lowers[head][i, i], 0.0).astype(BF16), low[head, i]).astype(BF16)
            for head, i in names
        }
        tri = {n: tri[n] - dot(low[n], inner[n]) for n in names}
        size *= 2
    tri = {n: tri[n].astype(BF16) for n in names}
    solved = [[] for _ in range(heads)]
    for i in range(parts):
        for head in range(heads):
            need = rhs[head][i * HALF : (i + 1) * HALF]
            for j in range(i):
                need = need - fine_dot(lowers[head][i, j], solved[head][j])
            solved[head].append(dot(tri[head, i], need.astype(BF16)))
    for head in range(heads):
        both = jnp.concatenate(solved[head], 0).astype(BF16)
        solved_out[head] = both
        ended = dot(ends[head], both)
        fade_end = fade[head : head + 1, rows - 1 : rows]
        own = jnp.concatenate([eye * fade_end - ended[:, :KD], ended[:, KD:]], 1)
        maps_out[head] = own


def front_kernel(
    place, qk, value, halo, hist_qk, hist_value, conv_qk, conv_value, rest, cols,
    maps_out, keys_out, solved_out, send_1, send_2, send_3, hist_s, conv_s, hist_v,
):
    heads = rest.shape[0]
    key_heads = heads // 2
    key_cols = qk.shape[2]
    taps = conv_value.shape[0]
    count = taps - 1
    first = place["seq"] == 0
    load_small(hist_qk, conv_qk, 1, hist_s, conv_s)
    hist_v[HALO - count :, :] = hist_value[...].astype(F32)
    for pair in range(key_heads):
        lanes = slice(pair * KD, (pair + 1) * KD)
        halo_lanes = slice(key_cols + pair * KD, key_cols + (pair + 1) * KD)
        key = unit_rows(
            front_rows(
                qk[1, :HALO, lanes], halo, hist_s, conv_s[:, lanes], lanes, halo_lanes, first
            )
        )
        keys = [key[i : i + 1] for i in range(count)]
        keys_out[pair] = stacked(keys, KD)
        dots = {
            (i, j): jnp.sum(keys[i] * keys[j], axis=-1, keepdims=True)
            for i in range(count)
            for j in range(i)
        }
        for head in (2 * pair, 2 * pair + 1):
            lanes = slice(head * DV, (head + 1) * DV)
            halo_lanes = slice(2 * key_cols + head * DV, 2 * key_cols + (head + 1) * DV)
            val = front_rows(
                value[:HALO, lanes], halo, hist_v, conv_value[:, lanes].astype(F32), lanes,
                halo_lanes, first,
            )
            beta = cols[:HALO, 4 * heads + head : 4 * heads + head + 1]
            cumul = running(cols[:HALO, 5 * heads + head : 5 * heads + head + 1], count)
            solved = []
            for i in range(count):
                need = jnp.concatenate([jnp.exp(cumul[i]) * keys[i], val[i : i + 1]], 1)
                for j in range(i):
                    need = need - (jnp.exp(cumul[i] - cumul[j]) * dots[i, j]) * solved[j]
                solved.append(beta[i : i + 1] * need)
            solved_out[head] = stacked(solved, KD + DV)
            ends = stacked([jnp.exp(cumul[-1] - cumul[i]) * keys[i] for i in range(count)], KD)
            maps_out[head] = put_ahead(rest[head], jnp.exp(cumul[-1]), ends, solved_out[head]).astype(BF16)
    for other, send in ((1, send_1), (2, send_2), (3, send_3)):
        send[...] = maps_out[pl.ds((place["member"] ^ other) * (heads // 4), heads // 4)]


def put_ahead(rest, fade, ends, solved):
    through = dot_nt(rest[:, :KD].astype(BF16), ends.astype(BF16)).astype(BF16)
    moved = dot(through, solved.astype(BF16))
    return jnp.concatenate([fade * rest[:, :KD] - moved[:, :KD], rest[:, KD:] + moved[:, KD:]], 1)


def query_kernel(
    place, qk, halo, hist_qk, conv_qk, keys, solved, cumul, cols, front_keys, front_solved,
    reads_out, local_out, hist_s, conv_s,
):
    heads, rows = cumul.shape
    key_heads = heads // 2
    count = conv_qk.shape[0] - 1
    first = place["seq"] == 0
    load_small(hist_qk, conv_qk, 0, hist_s, conv_s)
    line = lax.broadcasted_iota(jnp.int32, (rows, rows), 0)
    across = lax.broadcasted_iota(jnp.int32, (rows, rows), 1)
    within = line >= across
    in_front = lax.broadcasted_iota(jnp.int32, (HALO, 1), 0) < count
    zero = jnp.zeros((HALO, KD), F32)
    for pair in range(key_heads):
        lanes = slice(pair * KD, (pair + 1) * KD)
        query = unit_rows(conv_rows(qk[0, :, lanes].astype(F32), zero, conv_s[:, lanes]))
        query = query * (KD**-0.5)
        ahead = unit_rows(
            front_rows(qk[0, :HALO, lanes], halo, hist_s, conv_s[:, lanes], lanes, lanes, first)
        ) * (KD**-0.5)
        dots = dot_nt(query.astype(BF16), keys[pair])
        front = [front_keys[pair, i : i + 1] for i in range(count)]
        for head in (2 * pair, 2 * pair + 1):
            col = cols[:, head : head + 1]
            fade = cols[:, 3 * heads + head : 3 * heads + head + 1]
            spread = jnp.exp(jnp.minimum(col - cumul[head : head + 1], 0.0))
            attend = jnp.where(within, spread * dots, 0.0).astype(BF16)
            part = dot(attend, solved[head])
            reads = jnp.concatenate([fade * query - part[:, :KD], part[:, KD:]], 1)
            sums = running(cols[:HALO, 5 * heads + head : 5 * heads + head + 1], count)
            ends = stacked([jnp.exp(sums[-1] - sums[i]) * front[i] for i in range(count)], KD)
            reads = put_ahead(reads, jnp.exp(sums[-1]), ends, front_solved[head])
            first_rows = []
            for i in range(count):
                asked = ahead[i : i + 1]
                row = jnp.concatenate([jnp.exp(sums[i]) * asked, jnp.zeros((1, DV), F32)], 1)
                for j in range(i + 1):
                    weight = jnp.exp(sums[i] - sums[j]) * jnp.sum(
                        asked * front[j], axis=-1, keepdims=True
                    )
                    term = weight * front_solved[head, j : j + 1]
                    row = row + jnp.concatenate([-term[:, :KD], term[:, KD:]], 1)
                first_rows.append(row)
            top = jnp.where(in_front, stacked(first_rows, KD + DV), reads[:HALO])
            reads = jnp.concatenate([top, reads[HALO:]], 0)
            reads_out[head] = reads[:, :KD].astype(BF16)
            local_out[head] = reads[:, KD:]


def join(outer, inner):
    product = dot(outer[:, :KD], inner)
    return jnp.concatenate([product[:, :KD], product[:, KD:] + outer[:, KD:].astype(F32)], 1)


def act(outer, state):
    return dot(outer[:, :KD], state) + outer[:, KD:].astype(F32)


def in_order(bit, mine, other, body):
    @pl.when(bit == 1)
    def _():
        body(other, mine)

    @pl.when(bit == 0)
    def _():
        body(mine, other)


def each_member(member, body):
    for i in range(4):
        pl.when(member == i)(functools.partial(body, i))


def group_kernel(last, place, maps, got_1, got_2, got_3, state_in, total_out):
    size = got_1.shape[0]

    def body(member):
        mine = [maps[member * size + j] for j in range(size)]
        every = (mine, got_1, got_2, got_3)
        for j in range(size):
            if last:
                total_out[j] = state_in[member * size + j].astype(BF16)
            else:
                total_out[j] = every[member][j]
        for step in range(0 if last else 1, 4):
            for j in range(size):
                apply = act if last else join
                total_out[j] = apply(every[step ^ member][j], total_out[j]).astype(BF16)

    each_member(place["member"], body)


def level_kernel(level, last, *refs):
    if level == 2:
        place, total, received, state_in, total_out, prefix_out = refs
        prefix = None
    else:
        place, total, received, prefix, state_in, total_out, prefix_out = refs
    size = total.shape[0]
    bit = place[level]

    def body(low, high):
        for j in range(size):
            if last:
                state = state_in[place["member"] * size + j].astype(BF16)
                total_out[j] = act(high[j], act(low[j], state).astype(BF16)).astype(BF16)
            else:
                total_out[j] = join(high[j], low[j]).astype(BF16)

    in_order(bit, total, received, body)

    @pl.when(bit == 1)
    def _():
        for j in range(size):
            if prefix is None:
                prefix_out[j] = received[j]
            else:
                prefix_out[j] = join(prefix[j], received[j]).astype(BF16)

    @pl.when(bit == 0)
    def _():
        line = lax.broadcasted_iota(jnp.int32, (KD, KD + DV), 0)
        across = lax.broadcasted_iota(jnp.int32, (KD, KD + DV), 1)
        same = jnp.where(line == across, 1.0, 0.0).astype(BF16)
        for j in range(size):
            prefix_out[j] = same if prefix is None else prefix[j]


def enter_kernel(place, maps, got_1, got_2, got_3, state_in, came, *refs):
    *prefix, mine_out, send_1, send_2, send_3 = refs
    size = came.shape[0]
    outs = (mine_out, send_1, send_2, send_3)

    @pl.when(place["top"] == 1)
    def _():
        mine_out[...] = came[...]

    @pl.when(place["top"] == 0)
    def _():
        for j in range(size):
            mine_out[j] = state_in[place["member"] * size + j].astype(BF16)

    if prefix:
        for j in range(size):
            mine_out[j] = act(prefix[0][j], mine_out[j]).astype(BF16)

    def body(member):
        mine = [maps[member * size + j] for j in range(size)]
        every = (mine, got_1, got_2, got_3)
        states = [mine_out[j] for j in range(size)]
        for step in range(4):
            for j in range(size):
                outs[step ^ member][j] = states[j]
            if step < 3:
                states = [
                    act(every[step ^ member][j], states[j]).astype(BF16) for j in range(size)
                ]

    each_member(place["member"], body)


def normed_rows(local_part, reads, gate, gain, state):
    out = local_part + dot(reads, state)
    scale = lax.rsqrt(jnp.mean(out * out, axis=-1, keepdims=True) + 1e-06)
    return (out * scale * gain * silu(gate.astype(F32))).astype(BF16)


def normed_slots(slots, place, states, reads, local_reads, gate_z, gain, normed_out):
    size = states[0].shape[0]
    for at, slot in enumerate(slots):
        for j in range(size):
            head = (place["member"] ^ slot) * size + j
            normed_out[at, :, j * DV : (j + 1) * DV] = normed_rows(
                local_reads[head], reads[head], gate_z[:, lane_block(head, DV)], gain[...],
                states[at][j],
            )


def project(slots, place, normed, w_out, lift, width, j, target):
    depth = normed.shape[2]
    column = place["core"] if target else 1 - place["core"]
    lanes = lane_block(2 * (2 * j + lift) + column, width)
    total = None
    for at, slot in enumerate(slots):
        rows_of = lane_block(place["member"] ^ slot, depth)
        product = dot(normed[at], w_out[rows_of, lanes])
        total = product if total is None else total + product
    return total


def early_kernel(slots, place, *refs):
    *states, reads, local_reads, gate_z, gain, normed_out = refs
    normed_slots(slots, place, states, reads, local_reads, gate_z, gain, normed_out)


def both_products(early, late, place, early_rows, late_rows, w_out, lift, width, j, target):
    return project(early, place, early_rows, w_out, lift, width, j, target) + project(
        late, place, late_rows, w_out, lift, width, j, target
    )


def late_kernel(early, late, place, *refs):
    *states, reads, local_reads, gate_z, gain, early_rows, w_out = refs[:-3]
    late_rows, send_out, keep_out = refs[-3:]
    normed_slots(late, place, states, reads, local_reads, gate_z, gain, late_rows)
    for target, out in enumerate((send_out, keep_out)):
        for j in range(out.shape[0]):
            out[j] = both_products(
                early, late, place, early_rows, late_rows, w_out, 1 - place["lift"], out.shape[2],
                j, target,
            ).astype(BF16)


def home_kernel(
    early, late, place, early_rows, late_rows, w_out, maps, state_0, state_1, state_2, state_3,
    send_out, keep_out, checkpoint,
):
    for target, out in enumerate((send_out, keep_out)):
        for j in range(out.shape[0]):
            total = both_products(
                early, late, place, early_rows, late_rows, w_out, place["lift"], out.shape[2],
                j, target,
            )
            out[j] = total.astype(BF16)
    size = state_0.shape[0]
    for slot, states in enumerate((state_0, state_1, state_2, state_3)):
        for j in range(size):
            head = (place["member"] ^ slot) * size + j
            checkpoint[0, head] = act(maps[head], states[j])


def swapped(value, axis, step):
    count = lax.axis_size(axis)
    return lax.ppermute(value, axis, [(i, i ^ step) for i in range(count)])


def local(
    hidden_in, w_qk, w_value, w_outgate, w_ba, conv_qk, conv_value, hist_qk, hist_value,
    a_log, dt_bias, beta_bias, state_in, norm_gain, w_out,
):
    rows, width = hidden_in.shape
    key_cols = w_qk.shape[2]
    heads = a_log.shape[0]
    half = heads // 2
    taps = conv_value.shape[0]
    n_seq = lax.axis_size("seq")
    n_head = lax.axis_size("head")
    levels = n_seq.bit_length() - 1
    seq = lax.axis_index("seq")
    col = lax.axis_index("head")

    def scalar(value):
        return value.astype(jnp.int32).reshape(1)

    place = {i: scalar((seq >> i) & 1) for i in range(levels)} | {
        "seq": scalar(seq),
        "member": scalar(seq & 3),
        "top": scalar(seq >> (levels - 1)),
        "core": scalar(col & 1),
        "lift": scalar((col >> 1) & 1),
    }

    def only(*names):
        return {name: place[name] for name in names}


    qk = jnp.einsum("td,dce->cte", hidden_in, w_qk, preferred_element_type=F32).astype(BF16)
    value = jnp.dot(hidden_in, w_value, preferred_element_type=F32).astype(BF16)
    tail = rows - TAIL
    ends = jnp.concatenate([qk[0, tail:], qk[1, tail:], value[tail:]], 1)
    halo = lax.ppermute(ends, "seq", [(i, (i + 1) % n_seq) for i in range(n_seq)])
    gates = jnp.einsum("td,dch->cht", hidden_in, w_ba, preferred_element_type=F32).astype(BF16)

    small = [pltpu.VMEM((HALO, key_cols), F32), pltpu.VMEM((taps, key_cols), F32)]

    size = heads // 4
    keys, solved, rest, cumul, cols = call(
        prepare_kernel,
        (
            shape((half, rows, KD), BF16),
            shape((heads, rows, KD + DV), BF16),
            shape((heads, KD, KD + DV), F32),
            shape((heads, rows), F32),
            shape((rows, 128), F32),
        ),
        [VMEM] * 8,
        10000000,
        25165824,
        small[1:],
    )(
        a_log.reshape(1, heads), dt_bias.reshape(1, heads), beta_bias.reshape(1, heads),
        qk, value, gates, conv_qk, conv_value,
    )
    halo, rest = lax.optimization_barrier((halo, rest))
    map_shape = shape((size, KD, KD + DV), BF16)
    state_shape = shape((size, KD, DV), BF16)
    maps, front_keys, front_solved, *sends = call(
        front_kernel,
        (
            shape((heads, KD, KD + DV), BF16),
            shape((half, HALO, KD), F32),
            shape((heads, HALO, KD + DV), F32),
            map_shape,
            map_shape,
            map_shape,
        ),
        [VMEM] * 9,
        10000000,
        50331648,
        small + [pltpu.VMEM((HALO, heads * DV), F32)],
        only("seq", "member"),
    )(qk, value, halo, hist_qk, hist_value, conv_qk, conv_value, rest, cols)

    def to_all(values):
        got = {step: swapped(values[step - 1], "seq", step) for step in ORDER}
        return [got[step] for step in (1, 2, 3)]

    got = to_all(sends)
    later, _ = lax.optimization_barrier((qk, maps))
    reads = call(
        query_kernel,
        (shape((heads, rows, KD), BF16), shape((heads, rows, DV), F32)),
        [VMEM] * 10,
        100000000000,
        6291456,
        small,
        only("seq"),
    )(later, halo, hist_qk, conv_qk, keys, solved, cumul, cols, front_keys, front_solved)
    got, reads = lax.optimization_barrier((got, reads))

    last = levels == 3
    total = call(
        functools.partial(group_kernel, last),
        state_shape if last else map_shape,
        [VMEM] * 5,
        24000000000,
        50331648,
        flags=only("member"),
    )(maps, *got, state_in)
    prefix = ()
    for level in range(2, levels - 1):
        other = swapped(total, "seq", 1 << level)
        last = level == levels - 2
        total, prefix = call(
            functools.partial(level_kernel, level, last),
            (state_shape if last else map_shape, map_shape),
            [VMEM] * (3 if level == 2 else 4),
            10**8,
            1 << 20,
            flags=only("member", level),
        )(total, other, *prefix, state_in)
        prefix = (prefix,)
    came = swapped(total, "seq", 1 << (levels - 1))
    later, _ = lax.optimization_barrier((hidden_in, total))
    gate_z = jnp.dot(later, w_outgate, preferred_element_type=F32).astype(BF16)
    came, gate_z = lax.optimization_barrier((came, gate_z))
    mine, *sends = call(
        enter_kernel,
        (state_shape,) * 4,
        [VMEM] * (6 + len(prefix)),
        600000000,
        25165824,
        flags=only("member", "top"),
    )(maps, *got, state_in, came, *prefix)
    states = [mine] + to_all(sends)

    out_width = w_out.shape[1] // n_head
    blocks = n_head // 4
    side = only("member", "core", "lift")
    part_shape = shape((blocks, rows, out_width), BF16)
    early, late = (0,) + ORDER[:2], ORDER[2:]
    gain = norm_gain.reshape(1, DV)
    early_rows = call(
        functools.partial(early_kernel, early),
        shape((len(early), rows, size * DV), BF16),
        [VMEM] * (4 + len(early)),
        1000000,
        25165824,
        flags=side,
    )(*[states[slot] for slot in early], *reads, gate_z, gain)
    late_rows, send_out, keep = call(
        functools.partial(late_kernel, early, late),
        (shape((len(late), rows, size * DV), BF16), part_shape, part_shape),
        [VMEM] * (6 + len(late)),
        100000000000,
        50331648,
        flags=side,
    )(*[states[slot] for slot in late], *reads, gate_z, gain, early_rows, w_out)
    came_out = swapped(send_out, "head", 1)
    home_out, home_keep, checkpoint = call(
        functools.partial(home_kernel, early, late),
        (part_shape, part_shape, shape((1, heads, KD, DV), F32)),
        [VMEM] * 8,
        6000000000,
        25165824,
        flags=side,
    )(early_rows, late_rows, w_out, maps, *states)
    total_out = (keep.astype(F32) + came_out.astype(F32)).astype(BF16)
    came_far = swapped(total_out, "head", 2)
    came_home = swapped(home_out, "head", 1)
    mixed = home_keep.astype(F32) + came_home.astype(F32) + came_far.astype(F32)
    step = 4
    while step < n_head:
        here = (col // step) & 1
        blocks //= 2
        pairs = mixed.reshape(blocks, 2, rows, out_width)
        send_out = lax.dynamic_index_in_dim(pairs, 1 - here, 1, False).astype(BF16)
        mixed = lax.dynamic_index_in_dim(pairs, here, 1, False)
        mixed = mixed + swapped(send_out, "head", step).astype(F32)
        step *= 2
    return (mixed[0].astype(BF16), checkpoint)


def solution(mesh):
    return jax.shard_map(
        local,
        mesh=mesh,
        in_specs=(
            P("seq", None),
            P(None, None, "head"),
            P(None, "head"),
            P(None, "head"),
            P(None, None, "head"),
            P(None, None, "head"),
            P(None, "head"),
            P(None, None, "head"),
            P(None, "head"),
            P("head"),
            P("head"),
            P("head"),
            P("head", None, None),
            P(),
            P("head", None),
        ),
        out_specs=(P("seq", "head"), P("seq", "head", None, None)),
        check_vma=False,
    )
```
